32 devices in a mesh: seg: 4 (over y, x), chan: 8 (over z, core).
Axes of the slice: x: 2, y: 2, z: 4, core: 2. Of those that a mesh axis runs over, the one named last changes fastest.
Arguments:
- strain_rate: bfloat16 [48, 256, 4096], P('seg', None, 'chan'), may hold values from -6 to 6
- window_length: int32 [48], P('seg'), may hold values from 1024 to 4096, as said below
- source_channel: int32 [128], replicated, may hold values from 0 to 255, as said below
Outputs:
- stacked: float32 [256, 128, 512], P('chan', 'seg')
The draws below stay inside these ranges and needn't reach their ends.
Inputs may be any that keep to these rules, and one draw needn't show every extreme that they name: `window_length`: window 0 is fully recorded and window 1 holds exactly 1024 recorded samples. `source_channel`: the virtual sources are distinct channels; channel 0 and the last channel are always among them.
All inputs are finite; a program needn't handle non-finite values.
Results may differ from the reference program's by a relative error of at most 0.0045.
Values may be sent and summed in bfloat16 or wider, within the bound.
No kernel may reach another device: no remote copies, remote signals or barrier semaphores. Data moves between devices by JAX's collectives and lax.ppermute only.
A program may use at most 128 MiB of HBM per device.

```python
import math
import jax
import jax.numpy as jnp
from jax import lax

W = 4096
NF = 1152
FIRST_BIN = 16
SMOOTH = 64
MAXLAG = 256
VS = 128
SEGWIN = 12
CH_DEV = 32
LAGS = 512
CHANNELS = 256
WINDOWS = 48
N_SEG = 4


def draw_window_length(key, part):
    lengths = jax.random.randint(jax.random.fold_in(key, 11), (N_SEG * SEGWIN,), W // 4, W + 1)
    lengths = lengths.at[0].set(W)
    lengths = lengths.at[1].set(W // 4)
    return lengths.astype(jnp.int32)


def draw_source_channel(key, part):
    inner = jax.random.permutation(jax.random.fold_in(key, 21), CHANNELS - 2)[:VS - 2] + 1
    picked = jnp.concatenate([jnp.zeros((1,), jnp.int32), jnp.full((1,), CHANNELS - 1, jnp.int32), inner.astype(jnp.int32)])
    order = jax.random.permutation(jax.random.fold_in(key, 22), VS)
    return picked[order].astype(jnp.int32)


def block_scale(own_key, extent, cuts, smallest, top_value):
    loudness, own = 1.0, jax.random.fold_in(own_key, 6)
    for axis_at, parts in cuts:
        heights = jnp.exp(jax.random.uniform(jax.random.fold_in(own, axis_at), (parts,), jnp.float32, smallest / len(cuts), top_value / len(cuts)))
        loudness = loudness * jnp.repeat(heights, extent[axis_at] // parts).reshape([-1 if axis == axis_at else 1 for axis in range(len(extent))])
    return loudness


def centred(stream_key, dims, deviation, limit, shards=(), kind=jnp.bfloat16):
    drawn = deviation * jax.random.normal(stream_key, dims, jnp.float32)
    if shards:
        drawn = drawn * block_scale(stream_key, dims, shards, -0.22, 0.18)
    return jnp.clip(drawn, -limit, limit).astype(kind)


def setup_inputs(seed: int = 0) -> dict:
    key_of = jax.random.split(jax.random.key(seed), 4)
    strain_rate = centred(key_of[0], (WINDOWS, CHANNELS, W), 1.0, 6.0, ((0, 4), (2, 8)))
    window_length = draw_window_length(jax.random.fold_in(key_of[3], 71), 0)
    source_channel = draw_source_channel(jax.random.fold_in(key_of[3], 71), 0)
    return dict(strain_rate=strain_rate, window_length=window_length, source_channel=source_channel)


def angles(first, second):
    product = jnp.mod(first[:, None] * second[None, :], W)
    return product.astype(jnp.float32) * (2.0 * math.pi / W)

def forward_table():
    samples = jnp.arange(W, dtype=jnp.int32)
    freqs = FIRST_BIN + jnp.arange(NF, dtype=jnp.int32)
    phase = angles(samples, freqs)
    return jnp.concatenate([jnp.cos(phase), -jnp.sin(phase)], axis=1).astype(jnp.bfloat16)

def inverse_table():
    freqs = FIRST_BIN + jnp.arange(NF, dtype=jnp.int32)
    shifts = jnp.arange(LAGS, dtype=jnp.int32) - MAXLAG
    phase = angles(freqs, shifts)
    return jnp.concatenate([jnp.cos(phase), -jnp.sin(phase)], axis=0).astype(jnp.bfloat16)

def band_matrix():
    offsets = jnp.arange(NF, dtype=jnp.int32)
    nearby = jnp.abs(offsets[:, None] - offsets[None, :]) <= SMOOTH
    return (nearby.astype(jnp.bfloat16), lax.optimization_barrier(jnp.sum(nearby.astype(jnp.float32), axis=0)))

def whiten(signal, table, nearby, counts):
    spectrum = jnp.dot(signal, table, preferred_element_type=jnp.float32)
    spec_real = spectrum[:, :NF]
    spec_imag = spectrum[:, NF:]
    magnitude = jnp.sqrt(spec_real * spec_real + spec_imag * spec_imag).astype(jnp.bfloat16)
    smooth = jnp.dot(magnitude, nearby, preferred_element_type=jnp.float32) / counts + 1e-06
    return ((spec_real / smooth).astype(jnp.bfloat16), (spec_imag / smooth).astype(jnp.bfloat16))

def reference(strain_rate, window_length, source_channel):
    sample_index = jnp.arange(W, dtype=jnp.int32)
    inside = sample_index[None, :] < window_length[:, None]
    masked = jnp.where(inside[:, None, :], strain_rate, jnp.zeros((), jnp.bfloat16))
    grouped = masked.reshape(N_SEG, SEGWIN, CHANNELS, W)
    table = forward_table()
    lag_table = inverse_table()
    nearby, counts = band_matrix()

    def segment(carry, block):
        white_real, white_imag = whiten(block.reshape(SEGWIN * CHANNELS, W), table, nearby, counts)
        white_real = white_real.reshape(SEGWIN, CHANNELS, NF)
        white_imag = white_imag.reshape(SEGWIN, CHANNELS, NF)
        source_real = white_real[:, source_channel, :].astype(jnp.float32)
        source_imag = white_imag[:, source_channel, :].astype(jnp.float32)

        def correlate(start):
            part_real = lax.dynamic_slice_in_dim(white_real, start, CH_DEV, 1).astype(jnp.float32)
            part_imag = lax.dynamic_slice_in_dim(white_imag, start, CH_DEV, 1).astype(jnp.float32)
            cross_real = jnp.einsum('wck,wsk->csk', part_real, source_real) + jnp.einsum('wck,wsk->csk', part_imag, source_imag)
            cross_imag = jnp.einsum('wck,wsk->csk', part_imag, source_real) - jnp.einsum('wck,wsk->csk', part_real, source_imag)
            joined = jnp.concatenate([cross_real, cross_imag], axis=-1).astype(jnp.bfloat16)
            joined = joined.reshape(CH_DEV * VS, 2 * NF)
            return jnp.dot(joined, lag_table, preferred_element_type=jnp.float32).reshape(CH_DEV, VS, LAGS)
        starts = jnp.arange(CHANNELS // CH_DEV, dtype=jnp.int32) * CH_DEV
        blocks = lax.map(correlate, starts)
        return (carry + blocks.reshape(CHANNELS, VS, LAGS), None)
    summed, _ = lax.scan(segment, jnp.zeros((CHANNELS, VS, LAGS), jnp.float32), grouped)
    return summed * (1.0 / math.sqrt(NF * SEGWIN * N_SEG))
```

```python
import functools
import itertools
import math

import jax
import jax.numpy as jnp
import ml_dtypes
import numpy as np
from jax import lax
from jax.experimental import pallas as pl
from jax.experimental.pallas import tpu as pltpu
from jax.sharding import PartitionSpec as P

W = 4096
NF = 1152
FIRST_BIN = 16
SMOOTH = 64
MAXLAG = 256
LAGS = 512
RADIX = 8
PART = W // RADIX
TILE = 256
CLASSES = 4
BF16 = jnp.bfloat16
F32 = jnp.float32
VMEM_LIMIT = 60 * 1024 * 1024
GROUPS = ((0,), (4,), (2, 6), (1, 7), (3, 5))
COMPONENTS = ((0, 0), (4, 0), (2, 0), (2, 1), (1, 0), (1, 1), (3, 0), (3, 1))


def phases(first, second):
    product = np.mod(first[:, None].astype(np.int64) * second[None, :], W)
    return product.astype(np.float32) * np.float32(2.0 * math.pi / W)


@functools.lru_cache(maxsize=None)
def bin_order():
    residue = (FIRST_BIN + np.arange(NF)) % RADIX
    return np.concatenate([np.nonzero(residue == r)[0] for group in GROUPS for r in group])


@functools.lru_cache(maxsize=None)
def forward_blocks():
    order = bin_order()
    freqs = FIRST_BIN + order
    residue = freqs % RADIX
    phase = phases(np.arange(PART), freqs)
    cos, sin = np.cos(phase), np.sin(phase)
    base = np.minimum(residue, RADIX - residue)
    sign = np.where(residue == base, 1.0, -1.0).astype(np.float32)
    blocks, layout = [], []
    for begin in range(0, NF, TILE):
        end = min(begin + TILE, NF)
        used = []
        for index, (root, part) in enumerate(COMPONENTS):
            hit = (base[begin:end] == root).astype(np.float32)
            if not hit.any():
                continue
            c, s, g = cos[:, begin:end], sin[:, begin:end], sign[begin:end]
            real = c * hit if part == 0 else g * s * hit
            imag = -s * hit if part == 0 else g * c * hit
            block = np.zeros((PART, 2 * TILE), np.float32)
            block[:, : end - begin] = real
            block[:, TILE : TILE + end - begin] = imag
            used.append((index, len(blocks)))
            blocks.append(block)
        layout.append((begin, end, used))
    return np.stack(blocks).astype(ml_dtypes.bfloat16), layout


@functools.lru_cache(maxsize=None)
def band_tables():
    order = bin_order()
    nearby = np.abs(order[:, None] - order[None, :]) <= SMOOTH
    counts = nearby.sum(axis=0).astype(np.float32)
    return nearby.astype(ml_dtypes.bfloat16), (1.0 / counts)[None, :].astype(np.float32)


@functools.lru_cache(maxsize=None)
def lag_table():
    freqs = FIRST_BIN + bin_order()
    phase = phases(freqs, np.arange(LAGS) - MAXLAG)
    return np.concatenate([np.cos(phase), -np.sin(phase)], axis=0).astype(ml_dtypes.bfloat16)


def pack_kernel(lengths_ref, start_ref, x_ref, out_ref):
    core = lax.rem(pl.program_id(0), 2)
    windows, channels, samples = x_ref.shape
    half = channels // 2
    sample = start_ref[0] + lax.broadcasted_iota(jnp.int32, (half, samples), 1)
    for w in range(windows):
        inside = sample < lengths_ref[core * windows + w]
        for h in range(2):
            block = x_ref[w, h * half : (h + 1) * half, :]
            out_ref[0, h, w] = jnp.where(inside, block, jnp.zeros_like(block))


def pack(strain, lengths, start, chips):
    windows, channels, samples = strain.shape
    per_core = windows // 2
    chip_channels = channels // chips
    return pl.pallas_call(
        pack_kernel,
        grid=(2 * chips,),
        in_specs=[
            pl.BlockSpec(memory_space=pltpu.SMEM),
            pl.BlockSpec(memory_space=pltpu.SMEM),
            pl.BlockSpec((per_core, chip_channels, samples), lambda i: (i % 2, i // 2, 0)),
        ],
        out_specs=pl.BlockSpec(
            (1, 2, per_core, chip_channels // 2, samples), lambda i: (i, 0, 0, 0, 0)
        ),
        out_shape=jax.ShapeDtypeStruct(
            (2 * chips, 2, per_core, chip_channels // 2, samples), BF16
        ),
        compiler_params=pltpu.CompilerParams(vmem_limit_bytes=VMEM_LIMIT),
        name="pack",
    )(lengths, start, strain)


def transform_kernel(layout, x_ref, table_ref, nearby_ref, inverse_ref, select_ref,
                     white_ref, send_ref, parts, real, imag, white):
    slabs, rows, samples = x_ref.shape
    merge = PART // samples
    root = math.sqrt(0.5)
    step = 32

    def fold(i, carry):
        at = pl.ds(pl.multiple_of(i * step, step), step)
        x = []
        for a in range(RADIX):
            pieces = [x_ref[a * merge + j, at, :] for j in range(merge)]
            joined = pieces[0] if merge == 1 else jnp.concatenate(pieces, axis=-1)
            x.append(joined.astype(F32))
        s = [x[a] + x[a + 4] for a in range(4)]
        d = [x[a] - x[a + 4] for a in range(4)]
        even, odd = s[0] + s[2], s[1] + s[3]
        minus, plus = (d[1] - d[3]) * root, (d[1] + d[3]) * root
        values = (
            even + odd, even - odd, s[0] - s[2], s[3] - s[1],
            d[0] + minus, -(d[2] + plus), d[0] - minus, d[2] - plus,
        )
        for index, value in enumerate(values):
            parts[index, at, :] = value.astype(BF16)
        return carry

    lax.fori_loop(0, rows // step, fold, 0)
    for begin, end, used in layout:
        total = None
        for component, block in used:
            term = jnp.dot(parts[component], table_ref[block], preferred_element_type=F32)
            total = term if total is None else total + term
        real[:, begin:end] = total[:, : end - begin]
        imag[:, begin:end] = total[:, TILE : TILE + end - begin]
    re, im = real[...], imag[...]
    magnitude = jnp.sqrt(re * re + im * im).astype(BF16)
    smooth = jnp.dot(magnitude, nearby_ref[...], preferred_element_type=F32)
    inverse = 1.0 / (smooth * inverse_ref[...] + 1e-06)
    white[:, :NF] = (real[...] * inverse).astype(BF16)
    white[:, NF:] = (imag[...] * inverse).astype(BF16)
    half = rows // 2
    for h in range(2):
        white_ref[h] = white[h * half : (h + 1) * half, :]
    for q in range(select_ref.shape[0]):
        send_ref[q] = jnp.dot(
            select_ref[q], white[...], preferred_element_type=F32
        ).astype(BF16)


def transform(received, select):
    slabs, rows, samples = received.shape
    table, layout = forward_blocks()
    nearby, inverse = band_tables()
    classes, slots, _ = select.shape
    whole = pl.BlockSpec(memory_space=pltpu.VMEM)
    return pl.pallas_call(
        functools.partial(transform_kernel, layout),
        in_specs=[whole] * 5,
        out_specs=[whole, whole],
        out_shape=[
            jax.ShapeDtypeStruct((2, rows // 2, 2 * NF), BF16),
            jax.ShapeDtypeStruct((classes, slots, 2 * NF), BF16),
        ],
        scratch_shapes=[
            pltpu.VMEM((len(COMPONENTS), rows, PART), BF16),
            pltpu.VMEM((rows, NF), F32),
            pltpu.VMEM((rows, NF), F32),
            pltpu.VMEM((rows, 2 * NF), BF16),
        ],
        compiler_params=pltpu.CompilerParams(vmem_limit_bytes=VMEM_LIMIT),
        name="transform",
    )(received, table, nearby, inverse, select)


def correlate_kernel(segs, own_a_ref, own_b_ref, src_a_ref, src_b_ref, place_ref, table_ref,
                     out_ref, own_f, src_f, cross):
    half = own_a_ref.shape[0]
    channels = own_a_ref.shape[1]
    group = 8
    sources = segs * group
    for part, ref in enumerate((own_a_ref, own_b_ref)):
        for w in range(half):
            re = ref[w, :, :NF].astype(F32)
            im = ref[w, :, NF:].astype(F32)
            own_f[0, part * half + w] = re
            own_f[1, part * half + w] = im
            own_f[2, part * half + w] = re + im
    for part, ref in enumerate((src_a_ref, src_b_ref)):
        re = jnp.dot(place_ref[...], ref[:, :NF], preferred_element_type=F32)
        im = jnp.dot(place_ref[...], ref[:, NF:], preferred_element_type=F32)
        at = slice(part * half, (part + 1) * half)
        src_f[0, at] = re.reshape(half, sources, NF)
        src_f[1, at] = (re - im).reshape(half, sources, NF)
        src_f[2, at] = (re + im).reshape(half, sources, NF)

    tiles = NF // 128

    def channels_of(i, carry):
        eight = i // tiles
        begin = pl.multiple_of((i % tiles) * 128, 128)
        lanes = pl.ds(begin, 128)
        lanes_im = pl.ds(pl.multiple_of(NF + begin, 128), 128)
        base = pl.multiple_of(eight * 8, 8)
        for c in range(8):
            rows = pl.ds(pl.multiple_of((base + c) * group, group), group)
            mine = [
                [
                    jnp.broadcast_to(own_f[j, w, pl.ds(base, 8), lanes][c : c + 1], (group, 128))
                    for w in range(2 * half)
                ]
                for j in range(3)
            ]
            for g in range(segs):
                at = slice(g * group, (g + 1) * group)
                both = only_im = only_re = None
                for w in range(2 * half):
                    t0 = mine[2][w] * src_f[0, w, at, lanes]
                    t1 = mine[1][w] * src_f[1, w, at, lanes]
                    t2 = mine[0][w] * src_f[2, w, at, lanes]
                    both = t0 if both is None else both + t0
                    only_im = t1 if only_im is None else only_im + t1
                    only_re = t2 if only_re is None else only_re + t2
                cross[g, rows, lanes] = both - only_im
                cross[g, rows, lanes_im] = both - only_re
        return carry

    lax.fori_loop(0, (channels // 8) * tiles, channels_of, 0)
    for g in range(segs):
        out_ref[g] = jnp.dot(
            cross[g].astype(BF16), table_ref[...], preferred_element_type=F32
        ).astype(BF16)


def correlate(own_a, own_b, src_a, src_b, place, segs):
    half, channels, width = own_a.shape
    group = 8
    whole = pl.BlockSpec(memory_space=pltpu.VMEM)
    return pl.pallas_call(
        functools.partial(correlate_kernel, segs),
        in_specs=[whole] * 6,
        out_specs=whole,
        out_shape=jax.ShapeDtypeStruct((segs, channels * group, LAGS), BF16),
        scratch_shapes=[
            pltpu.VMEM((3, 2 * half, channels, NF), F32),
            pltpu.VMEM((3, 2 * half, segs * group, NF), F32),
            pltpu.VMEM((segs, channels * group, 2 * NF), F32),
        ],
        compiler_params=pltpu.CompilerParams(vmem_limit_bytes=VMEM_LIMIT),
        name="correlate",
    )(own_a, own_b, src_a, src_b, place, lag_table())


def finish_kernel(scale, place_ref, *refs):
    parts, out_ref = refs[:-1], refs[-1]
    segs = parts[0].shape[0]
    pairs = parts[0].shape[1] // 16
    block = out_ref.shape[1]

    def pair(i, carry):
        at = pl.ds(pl.multiple_of(i * 16, 16), 16)
        stacked = jnp.concatenate(
            [part[g, at, :] for g in range(segs) for part in parts], axis=0
        )
        total = jnp.dot(place_ref[...], stacked, preferred_element_type=F32) * scale
        out_ref[pl.ds(2 * i, 2)] = total.reshape(2, block, LAGS)
        return carry

    lax.fori_loop(0, pairs, pair, 0)


def finish(parts, place, scale, block):
    channels = parts[0].shape[1] // 8
    whole = pl.BlockSpec(memory_space=pltpu.VMEM)
    return pl.pallas_call(
        functools.partial(finish_kernel, scale),
        in_specs=[whole] * (1 + len(parts)),
        out_specs=whole,
        out_shape=jax.ShapeDtypeStruct((channels, block, LAGS), F32),
        compiler_params=pltpu.CompilerParams(vmem_limit_bytes=VMEM_LIMIT),
        name="finish",
    )(place, *parts)


def round_up(value, step):
    return -(-value // step) * step


def plan(source_channel, chips, chip_channels, segs):
    count = source_channel.shape[0]
    block = count // segs
    chip = source_channel // chip_channels
    index = jnp.arange(count, dtype=jnp.int32)
    seg = index // block
    same_seg = seg[:, None] == seg[None, :]
    earlier = index[None, :] < index[:, None]
    same_chip = chip[:, None] == chip[None, :]
    ahead = same_seg & ((chip[None, :] < chip[:, None]) | (same_chip & earlier))
    position = jnp.sum(ahead.astype(jnp.int32), axis=1)
    turns = np.array(
        [(0,) + t for t in itertools.product(range(CLASSES), repeat=segs - 1)], np.int32
    )
    turned = jnp.asarray(np.repeat(turns, block, axis=1))
    classes = (position[None, :] + turned) % CLASSES
    of_class = classes[:, None, :] == jnp.arange(CLASSES, dtype=jnp.int32)[None, :, None]
    of_chip = chip[:, None] == jnp.arange(chips, dtype=jnp.int32)[None, :]
    held = jnp.einsum(
        "rqs,sz->rqz", of_class.astype(BF16), of_chip.astype(BF16), preferred_element_type=F32
    )
    fullest = jnp.max(held, axis=(1, 2))
    best = jnp.argmin(fullest)
    chosen = lax.dynamic_index_in_dim(classes, best, 0, keepdims=False)
    same_class = chosen[:, None] == chosen[None, :]
    place = jnp.sum(
        (same_seg & same_class & (position[None, :] < position[:, None])).astype(jnp.int32), axis=1
    )
    slot = jnp.sum((same_chip & same_class & earlier).astype(jnp.int32), axis=1)
    return chip, chosen, place, slot, seg, jnp.min(fullest)


def on_device(strain_rate, window_length, source_channel):
    chan_index = lax.axis_index("chan")
    seg_index = lax.axis_index("seg")
    devices = lax.axis_size("chan")
    segs = lax.axis_size("seg")
    chips = devices // 2
    windows, all_channels, samples = strain_rate.shape
    channels = all_channels // devices
    per_core = windows // 2
    count = source_channel.shape[0]
    block = count // segs
    group = block // CLASSES
    my_chip = chan_index // 2
    my_core = chan_index % 2

    start = (chan_index * samples).astype(jnp.int32).reshape(1)
    packed = pack(strain_rate, window_length, start, chips)
    packed = packed.reshape(devices, 2 * per_core * channels, samples)
    received = lax.all_to_all(packed, "chan", split_axis=0, concat_axis=0, tiled=True)
    chip, chosen, place, slot, seg, fullest = plan(
        source_channel, chips, 2 * channels, segs
    )

    core_swap = [(i, i ^ 1) for i in range(devices)]
    upward = [(i, i + 2) for i in range(devices - 2)]
    downward = [(i + 2, i) for i in range(devices - 2)]

    row = np.arange(2 * per_core * channels)
    row_window = (row // channels) % per_core
    row_channel = (row // (per_core * channels)) * channels + row % channels
    kinds = jnp.arange(CLASSES, dtype=jnp.int32)
    spots = jnp.arange(group * segs, dtype=jnp.int32)
    spot_of_row = np.tile(np.arange(group * segs), per_core)
    window_of_row = np.repeat(np.arange(per_core), group * segs)

    def seated(cap):
        seats = round_up(per_core * cap, 16)
        seat = np.arange(seats)
        seat_window = np.where(seat < per_core * cap, seat // cap, -1).astype(np.int32)
        seat_slot = (seat % cap).astype(np.int32)

        def select(source_channel, chip, chosen, place, slot):
            sits = (
                (chosen[None, None, :] == kinds[:, None, None])
                & (slot[None, None, :] == jnp.arange(cap, dtype=jnp.int32)[None, :, None])
                & (chip[None, None, :] == my_chip)
            )
            local = source_channel % (2 * channels)
            held = jnp.sum(jnp.where(sits, local[None, None, :] + 1, 0), axis=-1) - 1
            return (
                (held[:, seat_slot][:, :, None] == row_channel[None, None, :])
                & (seat_window[:, None] == row_window[None, :])[None]
            ).astype(BF16)

        def where(chip, chosen, place, slot):
            at_spot = (
                (chosen[None, None, :] == kinds[:, None, None])
                & (seg * group + place == spots[:, None])[None]
            )
            spot_slot = jnp.sum(jnp.where(at_spot, slot[None, None, :], 0), axis=-1)
            spot_chip = jnp.sum(jnp.where(at_spot, chip[None, None, :], 0), axis=-1)
            spot_far = (spot_chip - my_chip) % chips
            far = np.repeat(np.arange(chips), seats).astype(np.int32)
            return (
                (spot_slot[:, spot_of_row][:, :, None] == np.tile(seat_slot, chips)[None, None, :])
                & (spot_far[:, spot_of_row][:, :, None] == far[None, None, :])
                & (window_of_row[:, None] == np.tile(seat_window, chips)[None, :])[None]
            ).astype(BF16)

        def gather(send):
            from_below, from_above = [None] * chips, [None] * chips
            up = down = send
            for hop in range(1, chips):
                up = lax.ppermute(up, "chan", upward)
                down = lax.ppermute(down, "chan", downward)
                from_below[hop], from_above[hop] = up, down
            merged = [send]
            for far_by in range(1, chips):
                merged.append(from_above[far_by] + from_below[chips - far_by])
            return jnp.concatenate(merged, axis=0)

        return select, where, gather

    def summed():
        def select(source_channel, chip, chosen, place, slot):
            at_spot = (
                (chosen[None, None, :] == kinds[:, None, None])
                & (seg * group + place == spots[:, None])[None]
                & (chip == my_chip)[None, None, :]
            )
            local = source_channel % (2 * channels)
            held = jnp.sum(jnp.where(at_spot, local[None, None, :] + 1, 0), axis=-1) - 1
            return (
                (held[:, spot_of_row][:, :, None] == row_channel[None, None, :])
                & (window_of_row[:, None] == row_window[None, :])[None]
            ).astype(BF16)

        def where(chip, chosen, place, slot):
            same = np.eye(per_core * group * segs, dtype=np.float32)
            return jnp.broadcast_to(jnp.asarray(same, BF16), (CLASSES,) + same.shape)

        def gather(send):
            lines = [list(range(core, devices, 2)) for core in range(2)]
            return lax.psum(send, "chan", axis_index_groups=lines)

        return select, where, gather

    def rest(way, received, source_channel, chip, chosen, place, slot):
        select, where, gather = way
        white, sends = transform(received, select(source_channel, chip, chosen, place, slot))
        white = white.reshape(2, per_core, channels, 2 * NF)
        own = lax.dynamic_index_in_dim(white, my_core, 0, keepdims=False)
        other = lax.dynamic_index_in_dim(white, 1 - my_core, 0, keepdims=False)
        own_other = lax.ppermute(other, "chan", core_swap)
        spread = where(chip, chosen, place, slot)
        pieces = []
        for q in range(CLASSES):
            mine = gather(sends[q])
            theirs = lax.ppermute(mine, "chan", core_swap)
            lag = correlate(own, own_other, mine, theirs, spread[q], segs)
            pieces.append(lax.all_to_all(lag, "seg", split_axis=0, concat_axis=0, tiled=True))

        my_chosen = lax.dynamic_slice_in_dim(chosen, seg_index * block, block)
        my_place = lax.dynamic_slice_in_dim(place, seg_index * block, block)
        width = CLASSES * 2 * group
        column = np.arange(segs * width) % width
        row_pair = np.repeat(np.arange(2), block)
        final = (
            (jnp.tile(my_chosen, 2)[:, None] == (column // (2 * group))[None, :])
            & (jnp.tile(my_place, 2)[:, None] == (column % group)[None, :])
            & (row_pair[:, None] == (column // group % 2)[None, :])
        ).astype(BF16)
        scale = 1.0 / math.sqrt(NF * windows * segs)
        return finish(pieces, final, scale, block)

    mean = count / CLASSES / chips
    cap = math.ceil(mean + 0.7 * math.sqrt(mean))
    operands = (received, source_channel, chip, chosen, place, slot)
    return lax.cond(
        fullest <= cap,
        functools.partial(rest, seated(cap)),
        functools.partial(rest, summed()),
        *operands,
    )


def solution(mesh):
    in_specs = (P("seg", None, "chan"), P("seg"), P())
    out_specs = P("chan", "seg", None)
    return jax.shard_map(
        on_device, mesh=mesh, in_specs=in_specs, out_specs=out_specs, check_vma=False
    )
```

```python
import functools
import itertools
import math

import jax
import jax.numpy as jnp
import ml_dtypes
import numpy as np
from jax import lax
from jax.experimental import pallas as pl
from jax.experimental.pallas import tpu as pltpu
from jax.sharding import PartitionSpec as P

W = 4096
NF = 1152
FIRST_BIN = 16
SMOOTH = 64
MAXLAG = 256
LAGS = 512
RADIX = 8
PART = W // RADIX
TILE = 256
CLASSES = 2
BF16 = jnp.bfloat16
F32 = jnp.float32
VMEM_LIMIT = 60 * 1024 * 1024
GROUPS = ((0,), (4,), (2, 6), (1, 7), (3, 5))
COMPONENTS = ((0, 0), (4, 0), (2, 0), (2, 1), (1, 0), (1, 1), (3, 0), (3, 1))


def phases(first, second):
    product = np.mod(first[:, None].astype(np.int64) * second[None, :], W)
    return product.astype(np.float32) * np.float32(2.0 * math.pi / W)


@functools.lru_cache(maxsize=None)
def bin_order():
    residue = (FIRST_BIN + np.arange(NF)) % RADIX
    return np.concatenate([np.nonzero(residue == r)[0] for group in GROUPS for r in group])


@functools.lru_cache(maxsize=None)
def forward_blocks():
    order = bin_order()
    freqs = FIRST_BIN + order
    residue = freqs % RADIX
    phase = phases(np.arange(PART), freqs)
    cos, sin = np.cos(phase), np.sin(phase)
    base = np.minimum(residue, RADIX - residue)
    sign = np.where(residue == base, 1.0, -1.0).astype(np.float32)
    blocks, layout = [], []
    for begin in range(0, NF, TILE):
        end = min(begin + TILE, NF)
        used = []
        for index, (root, part) in enumerate(COMPONENTS):
            hit = (base[begin:end] == root).astype(np.float32)
            if not hit.any():
                continue
            c, s, g = cos[:, begin:end], sin[:, begin:end], sign[begin:end]
            real = c * hit if part == 0 else g * s * hit
            imag = -s * hit if part == 0 else g * c * hit
            block = np.zeros((PART, 2 * TILE), np.float32)
            block[:, : end - begin] = real
            block[:, TILE : TILE + end - begin] = imag
            used.append((index, len(blocks)))
            blocks.append(block)
        layout.append((begin, end, used))
    return np.stack(blocks).astype(ml_dtypes.bfloat16), layout


@functools.lru_cache(maxsize=None)
def band_tables():
    order = bin_order()
    nearby = np.abs(order[:, None] - order[None, :]) <= SMOOTH
    counts = nearby.sum(axis=0).astype(np.float32)
    return nearby.astype(ml_dtypes.bfloat16), (1.0 / counts)[None, :].astype(np.float32)


@functools.lru_cache(maxsize=None)
def lag_table():
    freqs = FIRST_BIN + bin_order()
    phase = phases(freqs, np.arange(LAGS) - MAXLAG)
    return np.concatenate([np.cos(phase), -np.sin(phase)], axis=0).astype(ml_dtypes.bfloat16)


def pack_kernel(lengths_ref, start_ref, x_ref, out_ref):
    core = lax.rem(pl.program_id(0), 2)
    windows, channels, samples = x_ref.shape
    half = channels // 2
    sample = start_ref[0] + lax.broadcasted_iota(jnp.int32, (half, samples), 1)
    for w in range(windows):
        inside = (sample < lengths_ref[core * windows + w]).astype(F32).astype(BF16)
        for h in range(2):
            out_ref[0, h, w] = x_ref[w, h * half : (h + 1) * half, :] * inside


def pack(strain, lengths, start, chips):
    windows, channels, samples = strain.shape
    per_core = windows // 2
    chip_channels = channels // chips
    return pl.pallas_call(
        pack_kernel,
        grid=(2 * chips,),
        in_specs=[
            pl.BlockSpec(memory_space=pltpu.SMEM),
            pl.BlockSpec(memory_space=pltpu.SMEM),
            pl.BlockSpec((per_core, chip_channels, samples), lambda i: (i % 2, i // 2, 0)),
        ],
        out_specs=pl.BlockSpec(
            (1, 2, per_core, chip_channels // 2, samples), lambda i: (i, 0, 0, 0, 0)
        ),
        out_shape=jax.ShapeDtypeStruct(
            (2 * chips, 2, per_core, chip_channels // 2, samples), BF16
        ),
        compiler_params=pltpu.CompilerParams(vmem_limit_bytes=VMEM_LIMIT),
        name="pack",
    )(lengths, start, strain)


def transform_kernel(layout, core_ref, x_ref, table_ref, nearby_ref, inverse_ref, select_ref,
                     white_ref, own_ref, other_ref, send_ref, spare_ref, parts, real, imag):
    del spare_ref
    slabs, rows, samples = x_ref.shape
    merge = PART // samples
    root = math.sqrt(0.5)
    step = 32

    def fold(i, carry):
        at = pl.ds(pl.multiple_of(i * step, step), step)
        x = []
        for a in range(RADIX):
            pieces = [x_ref[a * merge + j, at, :] for j in range(merge)]
            joined = pieces[0] if merge == 1 else jnp.concatenate(pieces, axis=-1)
            x.append(joined.astype(F32))
        s = [x[a] + x[a + 4] for a in range(4)]
        d = [x[a] - x[a + 4] for a in range(4)]
        even, odd = s[0] + s[2], s[1] + s[3]
        minus, plus = (d[1] - d[3]) * root, (d[1] + d[3]) * root
        values = (
            even + odd, even - odd, s[0] - s[2], s[3] - s[1],
            d[0] + minus, -(d[2] + plus), d[0] - minus, d[2] - plus,
        )
        for index, value in enumerate(values):
            parts[index, at, :] = value.astype(BF16)
        return carry

    lax.fori_loop(0, rows // step, fold, 0)
    for begin, end, used in layout:
        total = None
        for component, block in used:
            term = jnp.dot(parts[component], table_ref[block], preferred_element_type=F32)
            total = term if total is None else total + term
        real[:, begin:end] = total[:, : end - begin]
        imag[:, begin:end] = total[:, TILE : TILE + end - begin]
    re, im = real[...], imag[...]
    magnitude = jnp.sqrt(re * re + im * im).astype(BF16)
    smooth = jnp.dot(magnitude, nearby_ref[...], preferred_element_type=F32)
    inverse = 1.0 / (smooth * inverse_ref[...] + 1e-06)
    white_ref[:, :NF] = (real[...] * inverse).astype(BF16)
    white_ref[:, NF:] = (imag[...] * inverse).astype(BF16)
    half = rows // 2
    core = core_ref[0]
    own_ref[...] = white_ref[pl.ds(pl.multiple_of(core * half, half), half), :]
    other_ref[...] = white_ref[pl.ds(pl.multiple_of((1 - core) * half, half), half), :]
    lanes = send_ref.shape[2]
    for q in range(send_ref.shape[0]):
        chosen = jnp.dot(
            select_ref[q * lanes : (q + 1) * lanes, :], white_ref[...], preferred_element_type=F32
        )
        for begin in range(0, 2 * NF, 128):
            send_ref[q, begin : begin + 128, :] = jnp.transpose(
                chosen[:, begin : begin + 128]
            ).astype(BF16)


def transform(received, select, core, lanes, spare):
    slabs, rows, samples = received.shape
    table, layout = forward_blocks()
    nearby, inverse = band_tables()
    whole = pl.BlockSpec(memory_space=pltpu.VMEM)
    return pl.pallas_call(
        functools.partial(transform_kernel, layout),
        in_specs=[pl.BlockSpec(memory_space=pltpu.SMEM)] + [whole] * 5,
        out_specs=[whole] * 4 + [pl.BlockSpec(memory_space=pl.ANY)],
        out_shape=[
            jax.ShapeDtypeStruct((rows, 2 * NF), BF16),
            jax.ShapeDtypeStruct((rows // 2, 2 * NF), BF16),
            jax.ShapeDtypeStruct((rows // 2, 2 * NF), BF16),
            jax.ShapeDtypeStruct((CLASSES, 2 * NF, lanes), BF16),
            jax.ShapeDtypeStruct(spare, BF16),
        ],
        scratch_shapes=[
            pltpu.VMEM((len(COMPONENTS), rows, PART), BF16),
            pltpu.VMEM((rows, NF), F32),
            pltpu.VMEM((rows, NF), F32),
        ],
        compiler_params=pltpu.CompilerParams(vmem_limit_bytes=VMEM_LIMIT),
        name="transform",
    )(core, received, table, nearby, inverse, select)


def gather_bins_kernel(mine_ref, theirs_ref, out_ref):
    windows, channels, _ = mine_ref.shape
    lane = lax.broadcasted_iota(jnp.int32, (channels, 128), 1)
    upper = [((lane // (8 << bit)) % 2) == 1 for bit in range(4)]

    def turned(tiles):
        tiles = list(tiles)
        for bit in range(4):
            shift = 8 << bit
            for j in range(16):
                if (j >> bit) & 1:
                    continue
                low, high = tiles[j], tiles[j + (1 << bit)]
                if low is None and high is None:
                    continue
                zero = jnp.zeros((channels, 128), F32)
                low = zero if low is None else low
                high = zero if high is None else high
                tiles[j] = jnp.where(upper[bit], pltpu.roll(high, shift, 1), low)
                tiles[j + (1 << bit)] = jnp.where(
                    upper[bit], high, pltpu.roll(low, 128 - shift, 1)
                )
        return tiles

    def tile(i, carry):
        values = []
        for part in range(2):
            at = pl.ds(pl.multiple_of(part * NF + i * 128, 128), 128)
            for ref in (mine_ref, theirs_ref):
                values += [ref[w, :, at].astype(F32) for w in range(windows)]
        first = turned(values[:16])
        second = turned(values[16:] + [None] * (32 - len(values)))
        for g in range(16):
            out_ref[i * 16 + g, :, :128] = first[g]
            out_ref[i * 16 + g, :, 128:] = second[g]
        return carry

    lax.fori_loop(0, NF // 128, tile, 0)


def gather_bins(mine, theirs):
    windows, channels, _ = mine.shape
    whole = pl.BlockSpec(memory_space=pltpu.VMEM)
    return pl.pallas_call(
        gather_bins_kernel,
        in_specs=[whole] * 2,
        out_specs=whole,
        out_shape=jax.ShapeDtypeStruct((NF // 8, channels, TILE), F32),
        compiler_params=pltpu.CompilerParams(vmem_limit_bytes=VMEM_LIMIT),
        name="gather_bins",
    )(mine, theirs)


def correlate_kernel(segs, chunk, full_ref, own_ref, mine_ref, theirs_ref, place_ref, spot_ref,
                     order_ref, table_ref, extra_ref, out_ref, src, cross, spare, sem):
    channels = own_ref.shape[1]
    windows = place_ref.shape[1] // 128
    sources = 64
    low = lax.broadcasted_iota(jnp.int32, (NF, 128), 1) < sources

    def spread(part, values, places):
        for w in range(0, windows, 2):
            at = places[:, w * 128 : (w + 2) * 128]
            re = jnp.dot(values[:NF], at, preferred_element_type=F32)
            im = jnp.dot(values[NF:], at, preferred_element_type=F32)
            for e in range(2):
                r, i = re[:, e * 128 : (e + 1) * 128], im[:, e * 128 : (e + 1) * 128]
                src[part * windows + w + e] = jnp.where(low, r, -i)
                src[(2 + part) * windows + w + e] = jnp.where(low, i, r)

    @pl.when(full_ref[0] == 0)
    def _():
        for part, ref in enumerate((mine_ref, theirs_ref)):
            joined = jnp.concatenate([ref[d] for d in range(ref.shape[0])], axis=1)
            spread(part, joined, place_ref)

    @pl.when(full_ref[0] != 0)
    def _():
        for part in range(2):
            copy = pltpu.make_async_copy(extra_ref.at[chunk, part], spare, sem)
            copy.start()
            copy.wait()
            spread(part, spare[...], spot_ref)

    shape = (8, TILE)
    lane = lax.broadcasted_iota(jnp.int32, shape, 1)
    pick = (lane % 8 == lax.broadcasted_iota(jnp.int32, shape, 0)) & (lane < 32 * windows)
    under = lax.broadcasted_iota(jnp.int32, (16, 128), 1) < sources
    zeros = jnp.zeros((TILE - 32 * windows, 128), F32)

    def bins(i, carry):
        pair = []
        for e in range(2):
            g = 2 * i + e
            at = pl.ds(pl.multiple_of(g * 8, 8), 8)
            right = jnp.concatenate(
                [src[j, at, :] for j in range(4 * windows)] + [zeros], axis=0
            ).astype(BF16)
            own = own_ref[g]
            left = jnp.concatenate(
                [
                    jnp.where(pick, jnp.broadcast_to(own[c : c + 1, :], shape), 0.0)
                    for c in range(channels)
                ],
                axis=0,
            ).astype(BF16)
            pair.append(jnp.dot(left, right, preferred_element_type=F32))
        at = pl.ds(pl.multiple_of(i * 16, 16), 16)
        for c in range(0, channels, 2):
            t = [
                jnp.concatenate([p[(c + e) * 8 : (c + e + 1) * 8] for p in pair], axis=0)
                for e in range(2)
            ]
            re = jnp.where(under, t[0], pltpu.roll(t[1], sources, 1))
            im = jnp.where(under, pltpu.roll(t[0], sources, 1), t[1])
            lanes = slice((c % 4) * 64, (c % 4) * 64 + 128)
            cross[c // 4, 0, at, lanes] = re.astype(BF16)
            cross[c // 4, 1, at, lanes] = im.astype(BF16)
        return carry

    lax.fori_loop(0, NF // 16, bins, 0)

    rows = TILE // segs

    def lags(i, carry):
        lag = jnp.dot(table_ref[0], cross[i, 0], preferred_element_type=F32)
        lag = (lag + jnp.dot(table_ref[1], cross[i, 1], preferred_element_type=F32)).astype(BF16)
        turned = lax.dot_general(
            order_ref[...], lag, (((1,), (1,)), ((), ())), preferred_element_type=F32
        ).astype(BF16)
        at = pl.ds(pl.multiple_of(i * rows, rows), rows)
        for g in range(segs):
            out_ref[g, at, :] = turned[g * rows : (g + 1) * rows, :]
        return carry

    lax.fori_loop(0, channels // 4, lags, 0)


def correlate(chunk, full, own, mine, theirs, place, extra, segs):
    groups, channels, _ = own.shape
    windows = place.shape[1] // 128
    group = 64 // segs
    spot = np.zeros((windows, 64, windows, 2, 64), np.float32)
    for w in range(windows):
        spot[w, :, w] = np.eye(64)[:, None, :]
    spot = spot.reshape(windows * 64, windows * 128).astype(ml_dtypes.bfloat16)
    order = np.zeros((segs, 4, group, 4, segs, group), np.float32)
    for g, c, u in itertools.product(range(segs), range(4), range(group)):
        order[g, c, u, c, g, u] = 1
    order = order.reshape(256, 256).astype(ml_dtypes.bfloat16)
    table = np.ascontiguousarray(lag_table().reshape(2, NF, LAGS).transpose(0, 2, 1))
    whole = pl.BlockSpec(memory_space=pltpu.VMEM)
    return pl.pallas_call(
        functools.partial(correlate_kernel, segs, chunk),
        in_specs=[pl.BlockSpec(memory_space=pltpu.SMEM)]
        + [whole] * 7
        + [pl.BlockSpec(memory_space=pl.ANY)],
        out_specs=whole,
        out_shape=jax.ShapeDtypeStruct((segs, channels * group, LAGS), BF16),
        scratch_shapes=[
            pltpu.VMEM((4 * windows, NF, 128), F32),
            pltpu.VMEM((channels // 4, 2, NF, TILE), BF16),
            pltpu.VMEM(extra.shape[2:], BF16),
            pltpu.SemaphoreType.DMA,
        ],
        compiler_params=pltpu.CompilerParams(vmem_limit_bytes=VMEM_LIMIT),
        name="correlate",
    )(full, own, mine, theirs, place, spot, order, table, extra)


def finish_kernel(scale, place_ref, *refs):
    parts, out_ref = refs[:-1], refs[-1]
    segs = parts[0].shape[0]
    pairs = out_ref.shape[0] // 2
    rows = parts[0].shape[1] // pairs
    block = out_ref.shape[1]
    for i in range(pairs):
        stacked = jnp.concatenate(
            [part[g, i * rows : (i + 1) * rows, :] for g in range(segs) for part in parts], axis=0
        )
        total = jnp.dot(place_ref[...], stacked, preferred_element_type=F32) * scale
        out_ref[2 * i : 2 * i + 2] = total.reshape(2, block, LAGS)


def finish(parts, place, scale, block, channels):
    segs, rows, _ = parts[0].shape
    step = 8
    piece = pl.BlockSpec((segs, rows * step // channels, LAGS), lambda i: (0, i, 0))
    return pl.pallas_call(
        functools.partial(finish_kernel, scale),
        grid=(channels // step,),
        in_specs=[pl.BlockSpec(place.shape, lambda i: (0, 0))] + [piece] * len(parts),
        out_specs=pl.BlockSpec((step, block, LAGS), lambda i: (i, 0, 0)),
        out_shape=jax.ShapeDtypeStruct((channels, block, LAGS), F32),
        compiler_params=pltpu.CompilerParams(vmem_limit_bytes=VMEM_LIMIT),
        name="finish",
    )(place, *parts)


def round_up(value, step):
    return -(-value // step) * step


def plan(source_channel, chips, chip_channels, segs):
    count = source_channel.shape[0]
    block = count // segs
    chip = source_channel // chip_channels
    index = jnp.arange(count, dtype=jnp.int32)
    seg = index // block
    same_seg = seg[:, None] == seg[None, :]
    earlier = index[None, :] < index[:, None]
    same_chip = chip[:, None] == chip[None, :]
    ahead = same_seg & ((chip[None, :] < chip[:, None]) | (same_chip & earlier))
    position = jnp.sum(ahead.astype(jnp.int32), axis=1)
    turns = np.array(
        [(0,) + t for t in itertools.product(range(CLASSES), repeat=segs - 1)], np.int32
    )
    turned = jnp.asarray(np.repeat(turns, block, axis=1))
    classes = (position[None, :] + turned) % CLASSES
    of_class = classes[:, None, :] == jnp.arange(CLASSES, dtype=jnp.int32)[None, :, None]
    of_chip = chip[:, None] == jnp.arange(chips, dtype=jnp.int32)[None, :]
    held = jnp.einsum(
        "rqs,sz->rqz", of_class.astype(BF16), of_chip.astype(BF16), preferred_element_type=F32
    )
    fullest = jnp.max(held, axis=(1, 2))
    best = jnp.argmin(fullest)
    chosen = lax.dynamic_index_in_dim(classes, best, 0, keepdims=False)
    same_class = chosen[:, None] == chosen[None, :]
    place = jnp.sum(
        (same_seg & same_class & (position[None, :] < position[:, None])).astype(jnp.int32), axis=1
    )
    slot = jnp.sum((same_chip & same_class & earlier).astype(jnp.int32), axis=1)
    return chip, chosen, place, slot, seg, jnp.min(fullest)


def on_device(strain_rate, window_length, source_channel):
    chan_index = lax.axis_index("chan")
    seg_index = lax.axis_index("seg")
    devices = lax.axis_size("chan")
    segs = lax.axis_size("seg")
    chips = devices // 2
    windows, all_channels, samples = strain_rate.shape
    channels = all_channels // devices
    per_core = windows // 2
    count = source_channel.shape[0]
    block = count // segs
    group = block // CLASSES
    spots = segs * group
    my_chip = chan_index // 2
    my_core = (chan_index % 2).astype(jnp.int32).reshape(1)

    start = (chan_index * samples).astype(jnp.int32).reshape(1)
    packed = pack(strain_rate, window_length, start, chips)
    packed = packed.reshape(devices, 2 * per_core * channels, samples)
    received = lax.all_to_all(packed, "chan", split_axis=0, concat_axis=0, tiled=True)

    chip, chosen, place, slot, seg, fullest = plan(source_channel, chips, 2 * channels, segs)
    mean = count / CLASSES / chips
    cap = math.ceil(mean + 0.7 * math.sqrt(2 * mean))
    full = (fullest > cap).astype(jnp.int32)

    core_swap = [(i, i ^ 1) for i in range(devices)]
    upward = [(i, i + 2) for i in range(devices - 2)]
    downward = [(i + 2, i) for i in range(devices - 2)]
    lines = [list(range(core, devices, 2)) for core in range(2)]

    row = np.arange(2 * per_core * channels)
    row_window = (row // channels) % per_core
    row_channel = (row // (per_core * channels)) * channels + row % channels
    kinds = jnp.arange(CLASSES, dtype=jnp.int32)
    local = source_channel % (2 * channels)
    here = chip == my_chip

    lanes = round_up(per_core * cap, 128)
    seat = np.arange(lanes)
    seat_window = np.where(seat < per_core * cap, seat // cap, -1).astype(np.int32)
    seat_slot = (seat % cap).astype(np.int32)
    sits = (
        (chosen[None, None, :] == kinds[:, None, None])
        & (slot[None, None, :] == seat_slot[None, :, None])
        & here[None, None, :]
    )
    held = jnp.sum(jnp.where(sits, local[None, None, :] + 1, 0), axis=-1) - 1
    select = (
        (held[:, :, None] == row_channel[None, None, :])
        & (seat_window[:, None] == row_window[None, :])[None]
    ).astype(BF16).reshape(CLASSES * lanes, row.shape[0])

    spot_index = jnp.arange(spots, dtype=jnp.int32)
    at_spot = (
        (chosen[None, None, :] == kinds[:, None, None])
        & (seg * group + place == spot_index[:, None])[None]
    )
    spot_slot = jnp.sum(jnp.where(at_spot, slot[None, None, :], 0), axis=-1)
    spot_chip = jnp.sum(jnp.where(at_spot, chip[None, None, :], 0), axis=-1)
    spot_far = (spot_chip - my_chip) % chips
    column_window = np.repeat(np.arange(per_core), 2 * spots)
    far = np.repeat(np.arange(chips), lanes).astype(np.int32)
    placing = (
        (jnp.tile(spot_slot, (1, 2 * per_core))[:, None, :] == np.tile(seat_slot, chips)[None, :, None])
        & (jnp.tile(spot_far, (1, 2 * per_core))[:, None, :] == far[None, :, None])
        & (np.tile(seat_window, chips)[:, None] == column_window[None, :])[None]
    ).astype(BF16)

    my_chosen = lax.dynamic_slice_in_dim(chosen, seg_index * block, block)
    my_place = lax.dynamic_slice_in_dim(place, seg_index * block, block)
    width = CLASSES * 2 * group
    column = np.arange(segs * width) % width
    row_pair = np.repeat(np.arange(2), block)
    final = (
        (jnp.tile(my_chosen, 2)[:, None] == (column // (2 * group))[None, :])
        & (jnp.tile(my_place, 2)[:, None] == (column % group)[None, :])
        & (row_pair[:, None] == (column // group % 2)[None, :])
    ).astype(BF16)

    spare = (CLASSES, 2, 2 * NF, per_core * spots)
    white, own, other, sends, unused = transform(received, select, my_core, lanes, spare)

    def all_summed(white, unused):
        local_at = jnp.sum(jnp.where(at_spot & here, local[None, None, :] + 1, 0), axis=-1) - 1
        wanted = (
            (jnp.tile(local_at, (1, per_core))[:, :, None] == row_channel[None, None, :])
            & (np.repeat(np.arange(per_core), spots)[:, None] == row_window[None, :])[None]
        ).astype(BF16)
        mine = jnp.einsum("qsr,rk->qks", wanted, white, preferred_element_type=F32).astype(BF16)
        mine = lax.psum(mine, "chan", axis_index_groups=lines)
        theirs = lax.ppermute(mine, "chan", core_swap)
        return jnp.stack([mine, theirs], axis=1)

    extra = lax.cond(full > 0, all_summed, lambda white, unused: unused, white, unused)

    own_other = lax.ppermute(other, "chan", core_swap)
    shape = (per_core, channels, 2 * NF)
    bins = gather_bins(own.reshape(shape), own_other.reshape(shape))

    pieces = []
    for q in range(CLASSES):
        from_below, from_above = [None] * chips, [None] * chips
        up = down = sends[q]
        for hop in range(1, chips):
            up = lax.ppermute(up, "chan", upward)
            down = lax.ppermute(down, "chan", downward)
            from_below[hop], from_above[hop] = up, down
        merged = [sends[q]]
        for far_by in range(1, chips):
            merged.append(from_above[far_by] + from_below[chips - far_by])
        mine = jnp.stack(merged)
        theirs = lax.ppermute(mine, "chan", core_swap)
        lag = correlate(q, full.reshape(1), bins, mine, theirs, placing[q], extra, segs)
        pieces.append(lax.all_to_all(lag, "seg", split_axis=0, concat_axis=0, tiled=True))

    scale = 1.0 / math.sqrt(NF * windows * segs)
    return finish(pieces, final, scale, block, channels)


def solution(mesh):
    in_specs = (P("seg", None, "chan"), P("seg"), P())
    out_specs = P("chan", "seg", None)
    return jax.shard_map(
        on_device, mesh=mesh, in_specs=in_specs, out_specs=out_specs, check_vma=False
    )
```

```python
import functools
import itertools
import math

import jax
import jax.numpy as jnp
import ml_dtypes
import numpy as np
from jax import lax
from jax.experimental import pallas as pl
from jax.experimental.pallas import tpu as pltpu
from jax.sharding import PartitionSpec as P

W = 4096
NF = 1152
FIRST_BIN = 16
SMOOTH = 64
MAXLAG = 256
LAGS = 512
RADIX = 8
PART = W // RADIX
TILE = 256
CLASSES = 2
BF16 = jnp.bfloat16
F32 = jnp.float32
VMEM_LIMIT = 60 * 1024 * 1024
GROUPS = ((0,), (4,), (2, 6), (1, 7), (3, 5))
COMPONENTS = ((0, 0), (4, 0), (2, 0), (2, 1), (1, 0), (1, 1), (3, 0), (3, 1))


def phases(first, second):
    product = np.mod(first[:, None].astype(np.int64) * second[None, :], W)
    return product.astype(np.float32) * np.float32(2.0 * math.pi / W)


@functools.lru_cache(maxsize=None)
def bin_order():
    residue = (FIRST_BIN + np.arange(NF)) % RADIX
    return np.concatenate([np.nonzero(residue == r)[0] for group in GROUPS for r in group])


@functools.lru_cache(maxsize=None)
def forward_blocks():
    order = bin_order()
    freqs = FIRST_BIN + order
    residue = freqs % RADIX
    phase = phases(np.arange(PART), freqs)
    cos, sin = np.cos(phase), np.sin(phase)
    base = np.minimum(residue, RADIX - residue)
    sign = np.where(residue == base, 1.0, -1.0).astype(np.float32)
    blocks, layout = [], []
    for begin in range(0, NF, TILE):
        end = min(begin + TILE, NF)
        used = []
        for index, (root, part) in enumerate(COMPONENTS):
            hit = (base[begin:end] == root).astype(np.float32)
            if not hit.any():
                continue
            c, s, g = cos[:, begin:end], sin[:, begin:end], sign[begin:end]
            real = c * hit if part == 0 else g * s * hit
            imag = -s * hit if part == 0 else g * c * hit
            block = np.zeros((PART, 2 * TILE), np.float32)
            block[:, : end - begin] = real
            block[:, TILE : TILE + end - begin] = imag
            used.append((index, len(blocks)))
            blocks.append(block)
        layout.append((begin, end, used))
    return np.stack(blocks).astype(ml_dtypes.bfloat16), layout


@functools.lru_cache(maxsize=None)
def band_tables():
    order = bin_order()
    nearby = np.abs(order[:, None] - order[None, :]) <= SMOOTH
    counts = nearby.sum(axis=0).astype(np.float32)
    return nearby.astype(ml_dtypes.bfloat16), (1.0 / counts)[None, :].astype(np.float32)


@functools.lru_cache(maxsize=None)
def lag_table():
    freqs = FIRST_BIN + bin_order()
    phase = phases(freqs, np.arange(LAGS) - MAXLAG)
    return np.concatenate([np.cos(phase), -np.sin(phase)], axis=0).astype(ml_dtypes.bfloat16)


def pack_kernel(lengths_ref, start_ref, x_ref, out_ref):
    core = lax.rem(pl.program_id(0), 2)
    windows, channels, samples = x_ref.shape
    half = channels // 2
    sample = start_ref[0] + lax.broadcasted_iota(jnp.int32, (half, samples), 1)
    for w in range(windows):
        inside = (sample < lengths_ref[core * windows + w]).astype(F32).astype(BF16)
        for h in range(2):
            out_ref[0, h, w] = x_ref[w, h * half : (h + 1) * half, :] * inside


def pack(strain, lengths, start, chips):
    windows, channels, samples = strain.shape
    per_core = windows // 2
    chip_channels = channels // chips
    return pl.pallas_call(
        pack_kernel,
        grid=(2 * chips,),
        in_specs=[
            pl.BlockSpec(memory_space=pltpu.SMEM),
            pl.BlockSpec(memory_space=pltpu.SMEM),
            pl.BlockSpec((per_core, chip_channels, samples), lambda i: (i % 2, i // 2, 0)),
        ],
        out_specs=pl.BlockSpec(
            (1, 2, per_core, chip_channels // 2, samples), lambda i: (i, 0, 0, 0, 0)
        ),
        out_shape=jax.ShapeDtypeStruct(
            (2 * chips, 2, per_core, chip_channels // 2, samples), BF16
        ),
        compiler_params=pltpu.CompilerParams(vmem_limit_bytes=VMEM_LIMIT),
        name="pack",
    )(lengths, start, strain)


def transform_kernel(layout, core_ref, x_ref, table_ref, nearby_ref, inverse_ref, select_ref,
                     white_ref, own_ref, other_ref, send_ref, parts, real, imag):
    slabs, rows, samples = x_ref.shape
    merge = PART // samples
    root = math.sqrt(0.5)
    step = 32

    def fold(i, carry):
        at = pl.ds(pl.multiple_of(i * step, step), step)
        x = []
        for a in range(RADIX):
            pieces = [x_ref[a * merge + j, at, :] for j in range(merge)]
            joined = pieces[0] if merge == 1 else jnp.concatenate(pieces, axis=-1)
            x.append(joined.astype(F32))
        s = [x[a] + x[a + 4] for a in range(4)]
        d = [x[a] - x[a + 4] for a in range(4)]
        even, odd = s[0] + s[2], s[1] + s[3]
        minus, plus = (d[1] - d[3]) * root, (d[1] + d[3]) * root
        values = (
            even + odd, even - odd, s[0] - s[2], s[3] - s[1],
            d[0] + minus, -(d[2] + plus), d[0] - minus, d[2] - plus,
        )
        for index, value in enumerate(values):
            parts[index, at, :] = value.astype(BF16)
        return carry

    lax.fori_loop(0, rows // step, fold, 0)
    for begin, end, used in layout:
        total = None
        for component, block in used:
            term = jnp.dot(parts[component], table_ref[block], preferred_element_type=F32)
            total = term if total is None else total + term
        real[:, begin:end] = total[:, : end - begin]
        imag[:, begin:end] = total[:, TILE : TILE + end - begin]
    re, im = real[...], imag[...]
    magnitude = jnp.sqrt(re * re + im * im).astype(BF16)
    smooth = jnp.dot(magnitude, nearby_ref[...], preferred_element_type=F32)
    inverse = 1.0 / (smooth * inverse_ref[...] + 1e-06)
    white_ref[:, :NF] = (real[...] * inverse).astype(BF16)
    white_ref[:, NF:] = (imag[...] * inverse).astype(BF16)
    half = rows // 2
    core = core_ref[0]
    own_ref[...] = white_ref[pl.ds(pl.multiple_of(core * half, half), half), :]
    other_ref[...] = white_ref[pl.ds(pl.multiple_of((1 - core) * half, half), half), :]
    lanes = send_ref.shape[2]
    for q in range(send_ref.shape[0]):
        chosen = jnp.dot(
            select_ref[q * lanes : (q + 1) * lanes, :], white_ref[...], preferred_element_type=F32
        )
        for begin in range(0, 2 * NF, 128):
            send_ref[q, begin : begin + 128, :] = jnp.transpose(
                chosen[:, begin : begin + 128]
            ).astype(BF16)


def transform(received, select, core, lanes):
    slabs, rows, samples = received.shape
    table, layout = forward_blocks()
    nearby, inverse = band_tables()
    whole = pl.BlockSpec(memory_space=pltpu.VMEM)
    return pl.pallas_call(
        functools.partial(transform_kernel, layout),
        in_specs=[pl.BlockSpec(memory_space=pltpu.SMEM)] + [whole] * 5,
        out_specs=[whole] * 4,
        out_shape=[
            jax.ShapeDtypeStruct((rows, 2 * NF), BF16),
            jax.ShapeDtypeStruct((rows // 2, 2 * NF), BF16),
            jax.ShapeDtypeStruct((rows // 2, 2 * NF), BF16),
            jax.ShapeDtypeStruct((CLASSES, 2 * NF, lanes), BF16),
        ],
        scratch_shapes=[
            pltpu.VMEM((len(COMPONENTS), rows, PART), BF16),
            pltpu.VMEM((rows, NF), F32),
            pltpu.VMEM((rows, NF), F32),
        ],
        compiler_params=pltpu.CompilerParams(vmem_limit_bytes=VMEM_LIMIT),
        name="transform",
    )(core, received, table, nearby, inverse, select)


def gather_bins_kernel(mine_ref, theirs_ref, out_ref):
    windows, channels, _ = mine_ref.shape
    lane = lax.broadcasted_iota(jnp.int32, (channels, 128), 1)
    upper = [((lane // (8 << bit)) % 2) == 1 for bit in range(4)]

    def turned(tiles):
        tiles = list(tiles)
        for bit in range(4):
            shift = 8 << bit
            for j in range(16):
                if (j >> bit) & 1:
                    continue
                low, high = tiles[j], tiles[j + (1 << bit)]
                if low is None and high is None:
                    continue
                zero = jnp.zeros((channels, 128), F32)
                low = zero if low is None else low
                high = zero if high is None else high
                tiles[j] = jnp.where(upper[bit], pltpu.roll(high, shift, 1), low)
                tiles[j + (1 << bit)] = jnp.where(
                    upper[bit], high, pltpu.roll(low, 128 - shift, 1)
                )
        return tiles

    def tile(i, carry):
        values = []
        for part in range(2):
            at = pl.ds(pl.multiple_of(part * NF + i * 128, 128), 128)
            for ref in (mine_ref, theirs_ref):
                values += [ref[w, :, at].astype(F32) for w in range(windows)]
        first = turned(values[:16])
        second = turned(values[16:] + [None] * (32 - len(values)))
        for g in range(16):
            out_ref[i * 16 + g, :, :128] = first[g].astype(BF16)
            out_ref[i * 16 + g, :, 128:] = second[g].astype(BF16)
        return carry

    lax.fori_loop(0, NF // 128, tile, 0)


def gather_bins(mine, theirs):
    windows, channels, _ = mine.shape
    whole = pl.BlockSpec(memory_space=pltpu.VMEM)
    return pl.pallas_call(
        gather_bins_kernel,
        in_specs=[whole] * 2,
        out_specs=whole,
        out_shape=jax.ShapeDtypeStruct((NF // 8, channels, TILE), BF16),
        compiler_params=pltpu.CompilerParams(vmem_limit_bytes=VMEM_LIMIT),
        name="gather_bins",
    )(mine, theirs)


def correlate_kernel(segs, own_ref, mine_ref, theirs_ref, place_ref, order_ref, table_ref,
                     out_ref, src, cross):
    channels = own_ref.shape[1]
    windows = place_ref.shape[1] // 128
    sources = 64
    low = lax.broadcasted_iota(jnp.int32, (NF, 128), 1) < sources

    def spread(part, values, places):
        for w in range(0, windows, 2):
            at = places[:, w * 128 : (w + 2) * 128]
            re = jnp.dot(values[:NF], at, preferred_element_type=F32)
            im = jnp.dot(values[NF:], at, preferred_element_type=F32)
            for e in range(2):
                r, i = re[:, e * 128 : (e + 1) * 128], im[:, e * 128 : (e + 1) * 128]
                src[part * windows + w + e] = jnp.where(low, r, -i)
                src[(2 + part) * windows + w + e] = jnp.where(low, i, r)

    for part, ref in enumerate((mine_ref, theirs_ref)):
        joined = jnp.concatenate([ref[d] for d in range(ref.shape[0])], axis=1)
        spread(part, joined, place_ref)

    shape = (8, TILE)
    lane = lax.broadcasted_iota(jnp.int32, shape, 1)
    pick = (lane % 8 == lax.broadcasted_iota(jnp.int32, shape, 0)) & (lane < 32 * windows)
    under = lax.broadcasted_iota(jnp.int32, (16, 128), 1) < sources
    zeros = jnp.zeros((TILE - 32 * windows, 128), F32)

    def bins(i, carry):
        pair = []
        for e in range(2):
            g = 2 * i + e
            at = pl.ds(pl.multiple_of(g * 8, 8), 8)
            right = jnp.concatenate(
                [src[j, at, :] for j in range(4 * windows)] + [zeros], axis=0
            ).astype(BF16)
            own = own_ref[g].astype(F32)
            left = jnp.concatenate(
                [
                    jnp.where(pick, jnp.broadcast_to(own[c : c + 1, :], shape), 0.0)
                    for c in range(channels)
                ],
                axis=0,
            ).astype(BF16)
            pair.append(jnp.dot(left, right, preferred_element_type=F32))
        at = pl.ds(pl.multiple_of(i * 16, 16), 16)
        at_im = pl.ds(pl.multiple_of(NF + i * 16, 16), 16)
        for c in range(0, channels, 2):
            t = [
                jnp.concatenate([p[(c + e) * 8 : (c + e + 1) * 8] for p in pair], axis=0)
                for e in range(2)
            ]
            re = jnp.where(under, t[0], pltpu.roll(t[1], sources, 1))
            im = jnp.where(under, pltpu.roll(t[0], sources, 1), t[1])
            lanes = slice((c % 4) * 64, (c % 4) * 64 + 128)
            cross[c // 4, at, lanes] = re.astype(BF16)
            cross[c // 4, at_im, lanes] = im.astype(BF16)
        return carry

    lax.fori_loop(0, NF // 16, bins, 0, unroll=4)

    rows = TILE // segs

    def lags(i, carry):
        lag = jnp.dot(table_ref[...], cross[i], preferred_element_type=F32).astype(BF16)
        turned = lax.dot_general(
            order_ref[...], lag, (((1,), (1,)), ((), ())), preferred_element_type=F32
        ).astype(BF16)
        at = pl.ds(pl.multiple_of(i * rows, rows), rows)
        for g in range(segs):
            out_ref[g, at, :] = turned[g * rows : (g + 1) * rows, :]
        return carry

    lax.fori_loop(0, channels // 4, lags, 0)


def correlate(own, mine, theirs, place, segs):
    groups, channels, _ = own.shape
    windows = place.shape[1] // 128
    group = 64 // segs
    order = np.zeros((segs, 4, group, 4, segs, group), np.float32)
    for g, c, u in itertools.product(range(segs), range(4), range(group)):
        order[g, c, u, c, g, u] = 1
    order = order.reshape(256, 256).astype(ml_dtypes.bfloat16)
    table = np.ascontiguousarray(lag_table().T)
    whole = pl.BlockSpec(memory_space=pltpu.VMEM)
    return pl.pallas_call(
        functools.partial(correlate_kernel, segs),
        in_specs=[whole] * 6,
        out_specs=whole,
        out_shape=jax.ShapeDtypeStruct((segs, channels * group, LAGS), BF16),
        scratch_shapes=[
            pltpu.VMEM((4 * windows, NF, 128), F32),
            pltpu.VMEM((channels // 4, 2 * NF, TILE), BF16),
        ],
        compiler_params=pltpu.CompilerParams(vmem_limit_bytes=VMEM_LIMIT),
        name="correlate",
    )(own, mine, theirs, place, order, table)


def finish_kernel(scale, place_ref, *refs):
    parts, out_ref = refs[:-1], refs[-1]
    segs = parts[0].shape[0]
    pairs = out_ref.shape[0] // 2
    rows = parts[0].shape[1] // pairs
    block = out_ref.shape[1]
    for i in range(pairs):
        stacked = jnp.concatenate(
            [part[g, i * rows : (i + 1) * rows, :] for g in range(segs) for part in parts], axis=0
        )
        total = jnp.dot(place_ref[...], stacked, preferred_element_type=F32) * scale
        out_ref[2 * i : 2 * i + 2] = total.reshape(2, block, LAGS)


def finish(parts, place, scale, block, channels):
    segs, rows, _ = parts[0].shape
    step = 8
    piece = pl.BlockSpec((segs, rows * step // channels, LAGS), lambda i: (0, i, 0))
    return pl.pallas_call(
        functools.partial(finish_kernel, scale),
        grid=(channels // step,),
        in_specs=[pl.BlockSpec(place.shape, lambda i: (0, 0))] + [piece] * len(parts),
        out_specs=pl.BlockSpec((step, block, LAGS), lambda i: (i, 0, 0)),
        out_shape=jax.ShapeDtypeStruct((channels, block, LAGS), F32),
        compiler_params=pltpu.CompilerParams(vmem_limit_bytes=VMEM_LIMIT),
        name="finish",
    )(place, *parts)


def round_up(value, step):
    return -(-value // step) * step


def plan(source_channel, chips, chip_channels, segs):
    count = source_channel.shape[0]
    block = count // segs
    chip = source_channel // chip_channels
    index = jnp.arange(count, dtype=jnp.int32)
    seg = index // block
    same_seg = seg[:, None] == seg[None, :]
    earlier = index[None, :] < index[:, None]
    same_chip = chip[:, None] == chip[None, :]
    ahead = same_seg & ((chip[None, :] < chip[:, None]) | (same_chip & earlier))
    position = jnp.sum(ahead.astype(jnp.int32), axis=1)
    turns = np.array(
        [(0,) + t for t in itertools.product(range(CLASSES), repeat=segs - 1)], np.int32
    )
    turned = jnp.asarray(np.repeat(turns, block, axis=1))
    classes = (position[None, :] + turned) % CLASSES
    of_class = classes[:, None, :] == jnp.arange(CLASSES, dtype=jnp.int32)[None, :, None]
    of_chip = chip[:, None] == jnp.arange(chips, dtype=jnp.int32)[None, :]
    held = jnp.einsum(
        "rqs,sz->rqz", of_class.astype(BF16), of_chip.astype(BF16), preferred_element_type=F32
    )
    fullest = jnp.max(held, axis=(1, 2))
    best = jnp.argmin(fullest)
    chosen = lax.dynamic_index_in_dim(classes, best, 0, keepdims=False)
    same_class = chosen[:, None] == chosen[None, :]
    place = jnp.sum(
        (same_seg & same_class & (position[None, :] < position[:, None])).astype(jnp.int32), axis=1
    )
    slot = jnp.sum((same_chip & same_class & earlier).astype(jnp.int32), axis=1)
    return chip, chosen, place, slot, seg, jnp.min(fullest)


def on_device(strain_rate, window_length, source_channel):
    chan_index = lax.axis_index("chan")
    seg_index = lax.axis_index("seg")
    devices = lax.axis_size("chan")
    segs = lax.axis_size("seg")
    chips = devices // 2
    windows, all_channels, samples = strain_rate.shape
    channels = all_channels // devices
    per_core = windows // 2
    count = source_channel.shape[0]
    block = count // segs
    group = block // CLASSES
    spots = segs * group
    my_chip = chan_index // 2
    my_core = (chan_index % 2).astype(jnp.int32).reshape(1)

    start = (chan_index * samples).astype(jnp.int32).reshape(1)
    packed = pack(strain_rate, window_length, start, chips)
    packed = packed.reshape(devices, 2 * per_core * channels, samples)
    received = lax.all_to_all(packed, "chan", split_axis=0, concat_axis=0, tiled=True)

    chip, chosen, place, slot, seg, fullest = plan(source_channel, chips, 2 * channels, segs)
    lanes = round_up(per_core * -(-count // (CLASSES * chips)), 128)
    cap = lanes // per_core
    full = (fullest > cap).astype(jnp.int32)

    core_swap = [(i, i ^ 1) for i in range(devices)]
    upward = [(i, i + 2) for i in range(devices - 2)]
    downward = [(i + 2, i) for i in range(devices - 2)]
    lines = [list(range(core, devices, 2)) for core in range(2)]

    row = np.arange(2 * per_core * channels)
    row_window = (row // channels) % per_core
    row_channel = (row // (per_core * channels)) * channels + row % channels
    kinds = jnp.arange(CLASSES, dtype=jnp.int32)
    local = source_channel % (2 * channels)
    here = chip == my_chip

    seat = np.arange(lanes)
    seat_window = np.where(seat < per_core * cap, seat // cap, -1).astype(np.int32)
    seat_slot = (seat % cap).astype(np.int32)
    sits = (
        (chosen[None, None, :] == kinds[:, None, None])
        & (slot[None, None, :] == seat_slot[None, :, None])
        & here[None, None, :]
    )
    held = jnp.sum(jnp.where(sits, local[None, None, :] + 1, 0), axis=-1) - 1
    select = (
        (held[:, :, None] == row_channel[None, None, :])
        & (seat_window[:, None] == row_window[None, :])[None]
    ).astype(BF16).reshape(CLASSES * lanes, row.shape[0])

    spot_index = jnp.arange(spots, dtype=jnp.int32)
    at_spot = (
        (chosen[None, None, :] == kinds[:, None, None])
        & (seg * group + place == spot_index[:, None])[None]
    )
    spot_slot = jnp.sum(jnp.where(at_spot, slot[None, None, :], 0), axis=-1)
    spot_chip = jnp.sum(jnp.where(at_spot, chip[None, None, :], 0), axis=-1)
    spot_far = jnp.stack([(spot_chip[0] - my_chip) % chips, spot_chip[1]])
    column_window = np.repeat(np.arange(per_core), 2 * spots)
    far = np.repeat(np.arange(chips), lanes).astype(np.int32)
    placing = (
        (jnp.tile(spot_slot, (1, 2 * per_core))[:, None, :] == np.tile(seat_slot, chips)[None, :, None])
        & (jnp.tile(spot_far, (1, 2 * per_core))[:, None, :] == far[None, :, None])
        & (np.tile(seat_window, chips)[:, None] == column_window[None, :])[None]
    ).astype(BF16)

    my_chosen = lax.dynamic_slice_in_dim(chosen, seg_index * block, block)
    my_place = lax.dynamic_slice_in_dim(place, seg_index * block, block)
    width = CLASSES * 2 * group
    column = np.arange(segs * width) % width
    row_pair = np.repeat(np.arange(2), block)
    final = (
        (jnp.tile(my_chosen, 2)[:, None] == (column // (2 * group))[None, :])
        & (jnp.tile(my_place, 2)[:, None] == (column % group)[None, :])
        & (row_pair[:, None] == (column // group % 2)[None, :])
    ).astype(BF16)

    white, own, other, sends = transform(received, select, my_core, lanes)
    own_other = lax.ppermute(other, "chan", core_swap)
    shape = (per_core, channels, 2 * NF)
    bins = gather_bins(own.reshape(shape), own_other.reshape(shape))

    from_below, from_above = [None] * chips, [None] * chips
    up = down = sends[0]
    for hop in range(1, chips):
        up = lax.ppermute(up, "chan", upward)
        down = lax.ppermute(down, "chan", downward)
        if hop == 2:
            up, down, bins, second = lax.optimization_barrier((up, down, bins, sends[1]))
        from_below[hop], from_above[hop] = up, down
    second = lax.all_gather(second, "chan", axis_index_groups=lines)
    merged = [sends[0]]
    for far_by in range(1, chips):
        merged.append(from_above[far_by] + from_below[chips - far_by])

    def stacks(mine, places):
        theirs = lax.ppermute(mine, "chan", core_swap)
        return correlate(bins, mine, theirs, places, segs)

    scale = 1.0 / math.sqrt(NF * windows * segs)

    def finished(lags):
        pieces = [
            lax.all_to_all(lag, "seg", split_axis=0, concat_axis=0, tiled=True) for lag in lags
        ]
        return finish(pieces, final, scale, block, channels)

    first_lag = stacks(jnp.stack(merged), placing[0])
    first_lag, second = lax.optimization_barrier((first_lag, second))
    second_lag = stacks(second, placing[1])
    seated = finished([first_lag, second_lag])

    def add_unseated(total):
        out = slot >= cap
        at = jnp.sum(jnp.where(at_spot & here & out, local[None, None, :] + 1, 0), axis=-1) - 1
        wanted = (
            (jnp.tile(at, (1, per_core))[:, :, None] == row_channel[None, None, :])
            & (np.repeat(np.arange(per_core), spots)[:, None] == row_window[None, :])[None]
        ).astype(BF16)
        spot = np.zeros((per_core, spots, per_core, 2, spots), np.float32)
        for w in range(per_core):
            spot[w, :, w] = np.eye(spots)[:, None, :]
        spot = jnp.asarray(spot.reshape(per_core * spots, -1), BF16)
        lags = []
        for q in range(CLASSES):
            mine = jnp.einsum("sr,rk->ks", wanted[q], white, preferred_element_type=F32)
            mine = lax.psum(mine.astype(BF16), "chan", axis_index_groups=lines)
            lags.append(stacks(mine[None], spot))
        return total + finished(lags)

    _, stacked = lax.while_loop(
        lambda carry: carry[0] < full,
        lambda carry: (carry[0] + 1, add_unseated(carry[1])),
        (jnp.zeros((), jnp.int32), seated),
    )
    return stacked


def solution(mesh):
    in_specs = (P("seg", None, "chan"), P("seg"), P())
    out_specs = P("chan", "seg", None)
    return jax.shard_map(
        on_device, mesh=mesh, in_specs=in_specs, out_specs=out_specs, check_vma=False
    )
```

```python
import functools
import itertools
import math

import jax
import jax.numpy as jnp
import ml_dtypes
import numpy as np
from jax import lax
from jax.experimental import pallas as pl
from jax.experimental.pallas import tpu as pltpu
from jax.sharding import PartitionSpec as P

W = 4096
NF = 1152
FIRST_BIN = 16
SMOOTH = 64
MAXLAG = 256
LAGS = 512
RADIX = 8
PART = W // RADIX
TILE = 256
CLASSES = 2
BF16 = jnp.bfloat16
F32 = jnp.float32
VMEM_LIMIT = 60 * 1024 * 1024
GROUPS = ((0,), (4,), (2, 6), (1, 7), (3, 5))
COMPONENTS = {0: (0, None), 4: (1, None), 2: (2, 3), 1: (4, 5), 3: (6, 7)}


def phases(first, second):
    product = np.mod(first[:, None].astype(np.int64) * second[None, :], W)
    return product.astype(np.float32) * np.float32(2.0 * math.pi / W)


@functools.lru_cache(maxsize=None)
def bin_order():
    residue = (FIRST_BIN + np.arange(NF)) % RADIX
    return np.concatenate([np.nonzero(residue == r)[0] for group in GROUPS for r in group])


@functools.lru_cache(maxsize=None)
def forward_blocks():
    order = bin_order()
    freqs = FIRST_BIN + order
    residue = freqs % RADIX
    phase = phases(np.arange(PART), freqs)
    cos, sin = np.cos(phase), np.sin(phase)
    base = np.minimum(residue, RADIX - residue)
    sign = np.where(residue == base, 1.0, -1.0).astype(np.float32)
    blocks, layout = [], []
    for begin in range(0, NF, TILE):
        end = min(begin + TILE, NF)
        used = []
        for root, (real_part, imag_part) in COMPONENTS.items():
            hit = (base[begin:end] == root).astype(np.float32)
            if not hit.any():
                continue
            block = np.zeros((PART, 2 * TILE), np.float32)
            block[:, : end - begin] = cos[:, begin:end] * hit
            block[:, TILE : TILE + end - begin] = sin[:, begin:end] * hit
            used.append((real_part, imag_part, len(blocks)))
            blocks.append(block)
        layout.append((begin, end, used))
    return np.stack(blocks).astype(ml_dtypes.bfloat16), sign[None, :], layout


@functools.lru_cache(maxsize=None)
def band_tables():
    order = bin_order()
    nearby = np.abs(order[:, None] - order[None, :]) <= SMOOTH
    counts = nearby.sum(axis=0).astype(np.float32)
    return order.astype(np.float32), (1.0 / counts)[None, :].astype(np.float32)


@functools.lru_cache(maxsize=None)
def lag_table():
    freqs = FIRST_BIN + bin_order()
    phase = phases(freqs, np.arange(LAGS) - MAXLAG)
    return np.concatenate([np.cos(phase), -np.sin(phase)], axis=0).astype(ml_dtypes.bfloat16)


def pack_kernel(lengths_ref, start_ref, x_ref, out_ref):
    windows, channels, samples = x_ref.shape
    windows = windows // 2
    half = channels // 2
    sample = start_ref[0] + lax.broadcasted_iota(jnp.int32, (16, samples), 1)
    for core, w in itertools.product(range(2), range(windows)):
        inside = (sample < lengths_ref[core * windows + w]).astype(F32).astype(BF16)
        inside = jnp.concatenate([inside] * (half // 16), axis=0)
        for h in range(2):
            rows = slice(h * half, (h + 1) * half)
            out_ref[core, h, w] = x_ref[core * windows + w, rows, :] * inside


def pack(strain, lengths, start, chips):
    windows, channels, samples = strain.shape
    per_core = windows // 2
    chip_channels = channels // chips
    return pl.pallas_call(
        pack_kernel,
        grid=(chips,),
        in_specs=[
            pl.BlockSpec(memory_space=pltpu.SMEM),
            pl.BlockSpec(memory_space=pltpu.SMEM),
            pl.BlockSpec((windows, chip_channels, samples), lambda i: (0, i, 0)),
        ],
        out_specs=pl.BlockSpec(
            (2, 2, per_core, chip_channels // 2, samples), lambda i: (i, 0, 0, 0, 0)
        ),
        out_shape=jax.ShapeDtypeStruct(
            (2 * chips, 2, per_core, chip_channels // 2, samples), BF16
        ),
        compiler_params=pltpu.CompilerParams(vmem_limit_bytes=VMEM_LIMIT),
        name="pack",
    )(lengths, start, strain)


def transform_kernel(layout, core_ref, x_ref, table_hbm, sign_ref, bin_row_ref, bin_column_ref,
                     inverse_ref, select_ref,
                     own_ref, other_ref, *rest):
    send_refs = rest[:CLASSES]
    parts, real, imag, white_ref, table_ref, nearby_ref, sems = rest[CLASSES:]
    tiles = [(used[0][2], used[-1][2] + 1) for _, _, used in layout]
    copies = [
        pltpu.make_async_copy(table_hbm.at[a:b], table_ref.at[a:b], sems.at[i])
        for i, (a, b) in enumerate(tiles)
    ]
    for copy in copies:
        copy.start()
    slabs, rows, samples = x_ref.shape
    merge = PART // samples
    root = math.sqrt(0.5)
    step = 32

    def fold(i, carry):
        at = pl.ds(pl.multiple_of(i * step, step), step)
        x = []
        for a in range(RADIX):
            pieces = [x_ref[a * merge + j, at, :] for j in range(merge)]
            joined = pieces[0] if merge == 1 else jnp.concatenate(pieces, axis=-1)
            x.append(joined.astype(F32))
        s = [x[a] + x[a + 4] for a in range(4)]
        d = [x[a] - x[a + 4] for a in range(4)]
        even, odd = s[0] + s[2], s[1] + s[3]
        minus, plus = (d[1] - d[3]) * root, (d[1] + d[3]) * root
        values = (
            even + odd, even - odd, s[0] - s[2], s[3] - s[1],
            d[0] + minus, -(d[2] + plus), d[0] - minus, d[2] - plus,
        )
        for index, value in enumerate(values):
            parts[index, at, :] = value.astype(BF16)
        return carry

    for begin in range(0, NF, 128):
        gap = jnp.abs(bin_column_ref[begin : begin + 128, :] - bin_row_ref[...])
        nearby_ref[begin : begin + 128, :] = jnp.where(gap <= SMOOTH, 1.0, 0.0).astype(BF16)
    lax.fori_loop(0, rows // step, fold, 0)
    for copy, (begin, end, used) in zip(copies, layout):
        copy.wait()
        straight = crossed = None
        for real_part, imag_part, block in used:
            term = jnp.dot(parts[real_part], table_ref[block], preferred_element_type=F32)
            straight = term if straight is None else straight + term
            if imag_part is None:
                continue
            term = jnp.dot(parts[imag_part], table_ref[block], preferred_element_type=F32)
            crossed = term if crossed is None else crossed + term
        width = end - begin
        re, im = straight[:, :width], -straight[:, TILE : TILE + width]
        if crossed is not None:
            side = sign_ref[:, begin:end]
            re = re + crossed[:, TILE : TILE + width] * side
            im = im + crossed[:, :width] * side
        real[:, begin:end] = re
        imag[:, begin:end] = im
    re, im = real[...], imag[...]
    magnitude = jnp.sqrt(re * re + im * im).astype(BF16)
    smooth = jnp.dot(magnitude, nearby_ref[...], preferred_element_type=F32)
    inverse = 1.0 / (smooth * inverse_ref[...] + 1e-06)
    white_ref[:, :NF] = (real[...] * inverse).astype(BF16)
    white_ref[:, NF:] = (imag[...] * inverse).astype(BF16)
    half = rows // 2
    core = core_ref[0]
    own_ref[...] = white_ref[pl.ds(pl.multiple_of(core * half, half), half), :]
    other_ref[...] = white_ref[pl.ds(pl.multiple_of((1 - core) * half, half), half), :]
    lanes = send_refs[0].shape[1]
    for q, send_ref in enumerate(send_refs):
        chosen = jnp.dot(
            select_ref[q * lanes : (q + 1) * lanes, :], white_ref[...], preferred_element_type=F32
        )
        for begin in range(0, 2 * NF, 128):
            send_ref[begin : begin + 128, :] = jnp.transpose(
                chosen[:, begin : begin + 128]
            ).astype(BF16)


def transform(received, select, core, lanes):
    slabs, rows, samples = received.shape
    table, sign, layout = forward_blocks()
    bins, inverse = band_tables()
    whole = pl.BlockSpec(memory_space=pltpu.VMEM)
    return pl.pallas_call(
        functools.partial(transform_kernel, layout),
        in_specs=[pl.BlockSpec(memory_space=pltpu.SMEM), whole]
        + [pl.BlockSpec(memory_space=pl.ANY)]
        + [whole] * 5,
        out_specs=[whole] * (2 + CLASSES),
        out_shape=[
            jax.ShapeDtypeStruct((rows // 2, 2 * NF), BF16),
            jax.ShapeDtypeStruct((rows // 2, 2 * NF), BF16),
        ]
        + [jax.ShapeDtypeStruct((2 * NF, lanes), BF16)] * CLASSES,
        scratch_shapes=[
            pltpu.VMEM((RADIX, rows, PART), BF16),
            pltpu.VMEM((rows, NF), F32),
            pltpu.VMEM((rows, NF), F32),
            pltpu.VMEM((rows, 2 * NF), BF16),
            pltpu.VMEM(table.shape, BF16),
            pltpu.VMEM((NF, NF), BF16),
            pltpu.SemaphoreType.DMA((len(layout),)),
        ],
        compiler_params=pltpu.CompilerParams(vmem_limit_bytes=VMEM_LIMIT),
        name="transform",
    )(core, received, table, sign, bins[None, :], bins[:, None], inverse, select)


def gather_bins_kernel(mine_ref, theirs_ref, out_ref):
    windows, channels, _ = mine_ref.shape
    lane = lax.broadcasted_iota(jnp.int32, (channels, 128), 1)
    upper = [((lane // (8 << bit)) % 2) == 1 for bit in range(4)]

    def turned(tiles):
        tiles = list(tiles)
        for bit in range(4):
            shift = 8 << bit
            for j in range(16):
                if (j >> bit) & 1:
                    continue
                low, high = tiles[j], tiles[j + (1 << bit)]
                if low is None and high is None:
                    continue
                zero = jnp.zeros((channels, 128), F32)
                low = zero if low is None else low
                high = zero if high is None else high
                tiles[j] = jnp.where(upper[bit], pltpu.roll(high, shift, 1), low)
                tiles[j + (1 << bit)] = jnp.where(
                    upper[bit], high, pltpu.roll(low, 128 - shift, 1)
                )
        return tiles

    def tile(i, carry):
        values = []
        for part in range(2):
            at = pl.ds(pl.multiple_of(part * NF + i * 128, 128), 128)
            for ref in (mine_ref, theirs_ref):
                values += [ref[w, :, at].astype(F32) for w in range(windows)]
        first = turned(values[:16])
        second = turned(values[16:] + [None] * (32 - len(values)))
        for g in range(16):
            out_ref[i * 16 + g, :, :128] = first[g].astype(BF16)
            out_ref[i * 16 + g, :, 128:] = second[g].astype(BF16)
        return carry

    lax.fori_loop(0, NF // 128, tile, 0)


def gather_bins(mine, theirs):
    windows, channels, _ = mine.shape
    whole = pl.BlockSpec(memory_space=pltpu.VMEM)
    return pl.pallas_call(
        gather_bins_kernel,
        in_specs=[whole] * 2,
        out_specs=whole,
        out_shape=jax.ShapeDtypeStruct((NF // 8, channels, TILE), BF16),
        compiler_params=pltpu.CompilerParams(vmem_limit_bytes=VMEM_LIMIT),
        name="gather_bins",
    )(mine, theirs)


def correlate_kernel(segs, mine_hbm, theirs_hbm, own_hbm, table_hbm, place_ref, order_ref,
                     out_ref, src, cross, mine_ref, theirs_ref, own_ref, table_ref, sems):
    copies = [
        pltpu.make_async_copy(a, b, sems.at[i])
        for i, (a, b) in enumerate(
            (
                (mine_hbm, mine_ref),
                (theirs_hbm, theirs_ref),
                (own_hbm, own_ref),
                (table_hbm, table_ref),
            )
        )
    ]
    for copy in copies:
        copy.start()
    channels = own_ref.shape[1]
    windows = place_ref.shape[1] // 128
    sources = 64
    low = lax.broadcasted_iota(jnp.int32, (NF, 128), 1) < sources

    def spread(part, values, places):
        for w in range(0, windows, 2):
            at = places[:, w * 128 : (w + 2) * 128]
            re = jnp.dot(values[:NF], at, preferred_element_type=F32)
            im = jnp.dot(values[NF:], at, preferred_element_type=F32)
            for e in range(2):
                r, i = re[:, e * 128 : (e + 1) * 128], im[:, e * 128 : (e + 1) * 128]
                src[part * windows + w + e] = jnp.where(low, r, -i)
                src[(2 + part) * windows + w + e] = jnp.where(low, i, r)

    for part, ref in enumerate((mine_ref, theirs_ref)):
        copies[part].wait()
        joined = jnp.concatenate([ref[d] for d in range(ref.shape[0])], axis=1)
        spread(part, joined, place_ref)

    shape = (8, TILE)
    lane = lax.broadcasted_iota(jnp.int32, shape, 1)
    pick = (lane % 8 == lax.broadcasted_iota(jnp.int32, shape, 0)) & (lane < 32 * windows)
    under = lax.broadcasted_iota(jnp.int32, (16, 128), 1) < sources
    zeros = jnp.zeros((TILE - 32 * windows, 128), F32)

    def bins(i, carry):
        pair = []
        for e in range(2):
            g = 2 * i + e
            at = pl.ds(pl.multiple_of(g * 8, 8), 8)
            right = jnp.concatenate(
                [src[j, at, :] for j in range(4 * windows)] + [zeros], axis=0
            ).astype(BF16)
            own = own_ref[g].astype(F32)
            left = jnp.concatenate(
                [
                    jnp.where(pick, jnp.broadcast_to(own[c : c + 1, :], shape), 0.0)
                    for c in range(channels)
                ],
                axis=0,
            ).astype(BF16)
            pair.append(jnp.dot(left, right, preferred_element_type=F32))
        at = pl.ds(pl.multiple_of(i * 16, 16), 16)
        at_im = pl.ds(pl.multiple_of(NF + i * 16, 16), 16)
        for c in range(0, channels, 2):
            t = [
                jnp.concatenate([p[(c + e) * 8 : (c + e + 1) * 8] for p in pair], axis=0)
                for e in range(2)
            ]
            re = jnp.where(under, t[0], pltpu.roll(t[1], sources, 1))
            im = jnp.where(under, pltpu.roll(t[0], sources, 1), t[1])
            lanes = slice((c % 4) * 64, (c % 4) * 64 + 128)
            cross[c // 4, at, lanes] = re.astype(BF16)
            cross[c // 4, at_im, lanes] = im.astype(BF16)
        return carry

    copies[2].wait()
    lax.fori_loop(0, NF // 16, bins, 0, unroll=8)

    rows = TILE // segs

    def lags(i, carry):
        lag = jnp.concatenate(
            [
                jnp.dot(
                    table_ref[n : n + TILE, :], cross[i], preferred_element_type=F32
                ).astype(BF16)
                for n in range(0, LAGS, TILE)
            ],
            axis=0,
        )
        turned = lax.dot_general(
            order_ref[...], lag, (((1,), (1,)), ((), ())), preferred_element_type=F32
        ).astype(BF16)
        at = pl.ds(pl.multiple_of(i * rows, rows), rows)
        for g in range(segs):
            out_ref[g, at, :] = turned[g * rows : (g + 1) * rows, :]
        return carry

    copies[3].wait()
    lax.fori_loop(0, channels // 4, lags, 0)


def correlate(own, mine, theirs, place, segs):
    groups, channels, _ = own.shape
    windows = place.shape[1] // 128
    group = 64 // segs
    order = np.zeros((segs, 4, group, 4, segs, group), np.float32)
    for g, c, u in itertools.product(range(segs), range(4), range(group)):
        order[g, c, u, c, g, u] = 1
    order = order.reshape(256, 256).astype(ml_dtypes.bfloat16)
    table = np.ascontiguousarray(lag_table().T)
    whole = pl.BlockSpec(memory_space=pltpu.VMEM)
    return pl.pallas_call(
        functools.partial(correlate_kernel, segs),
        in_specs=[pl.BlockSpec(memory_space=pl.ANY)] * 4 + [whole] * 2,
        out_specs=whole,
        out_shape=jax.ShapeDtypeStruct((segs, channels * group, LAGS), BF16),
        scratch_shapes=[
            pltpu.VMEM((4 * windows, NF, 128), F32),
            pltpu.VMEM((channels // 4, 2 * NF, TILE), BF16),
            pltpu.VMEM(mine.shape, BF16),
            pltpu.VMEM(theirs.shape, BF16),
            pltpu.VMEM(own.shape, BF16),
            pltpu.VMEM(table.shape, BF16),
            pltpu.SemaphoreType.DMA((4,)),
        ],
        compiler_params=pltpu.CompilerParams(vmem_limit_bytes=VMEM_LIMIT),
        name="correlate",
    )(mine, theirs, own, table, place, order)


def finish_kernel(scale, place_ref, *refs):
    parts, out_ref = refs[:-1], refs[-1]
    segs = parts[0].shape[0]
    pairs = out_ref.shape[0] // 2
    rows = parts[0].shape[1] // pairs
    block = out_ref.shape[1]
    for i in range(pairs):
        stacked = jnp.concatenate(
            [part[g, i * rows : (i + 1) * rows, :] for g in range(segs) for part in parts], axis=0
        )
        total = jnp.dot(place_ref[...], stacked, preferred_element_type=F32) * scale
        out_ref[2 * i : 2 * i + 2] = total.reshape(2, block, LAGS)


def finish(parts, place, scale, block, channels):
    segs, rows, _ = parts[0].shape
    step = math.gcd(channels, 16)
    piece = pl.BlockSpec((segs, rows * step // channels, LAGS), lambda i: (0, i, 0))
    return pl.pallas_call(
        functools.partial(finish_kernel, scale),
        grid=(channels // step,),
        in_specs=[pl.BlockSpec(place.shape, lambda i: (0, 0))] + [piece] * len(parts),
        out_specs=pl.BlockSpec((step, block, LAGS), lambda i: (i, 0, 0)),
        out_shape=jax.ShapeDtypeStruct((channels, block, LAGS), F32),
        compiler_params=pltpu.CompilerParams(vmem_limit_bytes=VMEM_LIMIT),
        name="finish",
    )(place, *parts)


def round_up(value, step):
    return -(-value // step) * step


def plan(source_channel, chips, chip_channels, segs):
    count = source_channel.shape[0]
    block = count // segs
    chip = source_channel // chip_channels
    index = jnp.arange(count, dtype=jnp.int32)
    seg = index // block
    same_seg = seg[:, None] == seg[None, :]
    earlier = index[None, :] < index[:, None]
    same_chip = chip[:, None] == chip[None, :]
    ahead = same_seg & ((chip[None, :] < chip[:, None]) | (same_chip & earlier))
    position = jnp.sum(ahead.astype(jnp.int32), axis=1)
    turns = np.array(
        [(0,) + t for t in itertools.product(range(CLASSES), repeat=segs - 1)], np.int32
    )
    turned = jnp.asarray(np.repeat(turns, block, axis=1))
    classes = (position[None, :] + turned) % CLASSES
    of_class = classes[:, None, :] == jnp.arange(CLASSES, dtype=jnp.int32)[None, :, None]
    of_chip = chip[:, None] == jnp.arange(chips, dtype=jnp.int32)[None, :]
    held = jnp.einsum(
        "rqs,sz->rqz", of_class.astype(BF16), of_chip.astype(BF16), preferred_element_type=F32
    )
    fullest = jnp.max(held, axis=(1, 2))
    best = jnp.argmin(fullest)
    chosen = lax.dynamic_index_in_dim(classes, best, 0, keepdims=False)
    same_class = chosen[:, None] == chosen[None, :]
    place = jnp.sum(
        (same_seg & same_class & (position[None, :] < position[:, None])).astype(jnp.int32), axis=1
    )
    slot = jnp.sum((same_chip & same_class & earlier).astype(jnp.int32), axis=1)
    return chip, chosen, place, slot, seg, jnp.min(fullest)


def on_device(strain_rate, window_length, source_channel):
    chan_index = lax.axis_index("chan")
    seg_index = lax.axis_index("seg")
    devices = lax.axis_size("chan")
    segs = lax.axis_size("seg")
    chips = devices // 2
    windows, all_channels, samples = strain_rate.shape
    channels = all_channels // devices
    per_core = windows // 2
    count = source_channel.shape[0]
    block = count // segs
    group = block // CLASSES
    spots = segs * group
    my_chip = chan_index // 2
    my_core = (chan_index % 2).astype(jnp.int32).reshape(1)

    start = (chan_index * samples).astype(jnp.int32).reshape(1)
    packed = pack(strain_rate, window_length, start, chips)
    packed = packed.reshape(devices, 2 * per_core * channels, samples)
    received = lax.all_to_all(packed, "chan", split_axis=0, concat_axis=0, tiled=True)

    chip, chosen, place, slot, seg, fullest = plan(source_channel, chips, 2 * channels, segs)
    lanes = round_up(per_core * -(-count // (CLASSES * chips)), 128)
    cap = lanes // per_core
    full = (fullest > cap).astype(jnp.int32)

    core_swap = [(i, i ^ 1) for i in range(devices)]
    upward = [(i, i + 2) for i in range(devices - 2)]
    downward = [(i + 2, i) for i in range(devices - 2)]
    lines = [list(range(core, devices, 2)) for core in range(2)]

    row = np.arange(2 * per_core * channels)
    row_window = (row // channels) % per_core
    row_channel = (row // (per_core * channels)) * channels + row % channels
    kinds = jnp.arange(CLASSES, dtype=jnp.int32)
    local = source_channel % (2 * channels)
    here = chip == my_chip

    seat = np.arange(lanes)
    seat_window = np.where(seat < per_core * cap, seat // cap, -1).astype(np.int32)
    seat_slot = (seat % cap).astype(np.int32)
    sits = (
        (chosen[None, None, :] == kinds[:, None, None])
        & (slot[None, None, :] == seat_slot[None, :, None])
        & here[None, None, :]
    )
    held = jnp.sum(jnp.where(sits, local[None, None, :] + 1, 0), axis=-1) - 1
    select = (
        (held[:, :, None] == row_channel[None, None, :])
        & (seat_window[:, None] == row_window[None, :])[None]
    ).astype(BF16).reshape(CLASSES * lanes, row.shape[0])

    spot_index = jnp.arange(spots, dtype=jnp.int32)
    at_spot = (
        (chosen[None, None, :] == kinds[:, None, None])
        & (seg * group + place == spot_index[:, None])[None]
    )
    spot_slot = jnp.sum(jnp.where(at_spot, slot[None, None, :], 0), axis=-1)
    spot_chip = jnp.sum(jnp.where(at_spot, chip[None, None, :], 0), axis=-1)
    spot_far = jnp.stack([(spot_chip[0] - my_chip) % chips, spot_chip[1]])
    column_window = np.repeat(np.arange(per_core), 2 * spots)
    far = np.repeat(np.arange(chips), lanes).astype(np.int32)
    placing = (
        (jnp.tile(spot_slot, (1, 2 * per_core))[:, None, :] == np.tile(seat_slot, chips)[None, :, None])
        & (jnp.tile(spot_far, (1, 2 * per_core))[:, None, :] == far[None, :, None])
        & (np.tile(seat_window, chips)[:, None] == column_window[None, :])[None]
    ).astype(BF16)

    my_chosen = lax.dynamic_slice_in_dim(chosen, seg_index * block, block)
    my_place = lax.dynamic_slice_in_dim(place, seg_index * block, block)
    width = CLASSES * 2 * group
    column = np.arange(segs * width) % width
    row_pair = np.repeat(np.arange(2), block)
    final = (
        (jnp.tile(my_chosen, 2)[:, None] == (column // (2 * group))[None, :])
        & (jnp.tile(my_place, 2)[:, None] == (column % group)[None, :])
        & (row_pair[:, None] == (column // group % 2)[None, :])
    ).astype(BF16)

    own, other, *sends = transform(received, select, my_core, lanes)
    own_other = lax.ppermute(other, "chan", core_swap)
    shape = (per_core, channels, 2 * NF)
    bins = gather_bins(own.reshape(shape), own_other.reshape(shape))

    from_below, from_above = [None] * chips, [None] * chips
    up = down = sends[0]
    for hop in range(1, chips):
        up = lax.ppermute(up, "chan", upward)
        down = lax.ppermute(down, "chan", downward)
        if hop == 2:
            up, down, bins, second = lax.optimization_barrier((up, down, bins, sends[1]))
        from_below[hop], from_above[hop] = up, down
    second = lax.all_gather(second, "chan", axis_index_groups=lines)
    merged = [sends[0]]
    for far_by in range(1, chips):
        merged.append(from_above[far_by] + from_below[chips - far_by])

    def stacks(mine, places):
        theirs = lax.ppermute(mine, "chan", core_swap)
        return correlate(bins, mine, theirs, places, segs)

    scale = 1.0 / math.sqrt(NF * windows * segs)

    def finished(lags):
        pieces = [
            lax.all_to_all(lag, "seg", split_axis=0, concat_axis=0, tiled=True) for lag in lags
        ]
        return finish(pieces, final, scale, block, channels)

    first_lag = stacks(jnp.stack(merged), placing[0])
    first_lag, second = lax.optimization_barrier((first_lag, second))
    second_lag = stacks(second, placing[1])
    seated = finished([first_lag, second_lag])

    def add_unseated(turn, total):
        out = (slot >= cap) & (turn < full)
        at = jnp.sum(jnp.where(at_spot & here & out, local[None, None, :] + 1, 0), axis=-1) - 1
        wanted = (
            (jnp.tile(at, (1, per_core))[:, :, None] == row_channel[None, None, :])
            & (np.repeat(np.arange(per_core), spots)[:, None] == row_window[None, :])[None]
        ).astype(BF16)
        spot = np.zeros((per_core, spots, per_core, 2, spots), np.float32)
        for w in range(per_core):
            spot[w, :, w] = np.eye(spots)[:, None, :]
        spot = jnp.asarray(spot.reshape(per_core * spots, -1), BF16)
        first = my_core[0] == 0
        white = jnp.concatenate([jnp.where(first, own, other), jnp.where(first, other, own)])
        lags = []
        for q in range(CLASSES):
            mine = jnp.einsum("sr,rk->ks", wanted[q], white, preferred_element_type=F32)
            mine = lax.psum(mine.astype(BF16), "chan", axis_index_groups=lines)
            lags.append(stacks(mine[None], spot))
        return total + finished(lags)

    _, stacked = lax.while_loop(
        lambda carry: carry[0] < full,
        lambda carry: (carry[0] + 1, add_unseated(*carry)),
        (jnp.zeros((), jnp.int32), seated),
    )
    return stacked


def solution(mesh):
    in_specs = (P("seg", None, "chan"), P("seg"), P())
    out_specs = P("chan", "seg", None)
    return jax.shard_map(
        on_device, mesh=mesh, in_specs=in_specs, out_specs=out_specs, check_vma=False
    )
```

```python
import functools
import itertools
import math

import jax
import jax.numpy as jnp
import ml_dtypes
import numpy as np
from jax import lax
from jax.experimental import pallas as pl
from jax.experimental.pallas import tpu as pltpu
from jax.sharding import PartitionSpec as P

W = 4096
NF = 1152
FIRST_BIN = 16
SMOOTH = 64
MAXLAG = 256
LAGS = 512
RADIX = 8
PART = W // RADIX
TILE = 256
CLASSES = 2
BF16 = jnp.bfloat16
F32 = jnp.float32
VMEM_LIMIT = 60 * 1024 * 1024
GROUPS = ((0,), (4,), (2, 6), (1, 7), (3, 5))
COMPONENTS = {0: (0, None), 4: (1, None), 2: (2, 3), 1: (4, 5), 3: (6, 7)}


def phases(first, second):
    product = np.mod(first[:, None].astype(np.int64) * second[None, :], W)
    return product.astype(np.float32) * np.float32(2.0 * math.pi / W)


@functools.lru_cache(maxsize=None)
def bin_order():
    residue = (FIRST_BIN + np.arange(NF)) % RADIX
    return np.concatenate([np.nonzero(residue == r)[0] for group in GROUPS for r in group])


@functools.lru_cache(maxsize=None)
def forward_blocks():
    order = bin_order()
    freqs = FIRST_BIN + order
    residue = freqs % RADIX
    phase = phases(np.arange(PART), freqs)
    cos, sin = np.cos(phase), np.sin(phase)
    base = np.minimum(residue, RADIX - residue)
    sign = np.where(residue == base, 1.0, -1.0).astype(np.float32)
    blocks, layout = [], []
    for begin in range(0, NF, TILE):
        end = min(begin + TILE, NF)
        used = []
        for root, (real_part, imag_part) in COMPONENTS.items():
            hit = (base[begin:end] == root).astype(np.float32)
            if not hit.any():
                continue
            block = np.zeros((PART, 2 * TILE), np.float32)
            block[:, : end - begin] = cos[:, begin:end] * hit
            block[:, TILE : TILE + end - begin] = sin[:, begin:end] * hit
            used.append((real_part, imag_part, len(blocks)))
            blocks.append(block)
        layout.append((begin, end, used))
    return np.stack(blocks).astype(ml_dtypes.bfloat16), sign[None, :], layout


@functools.lru_cache(maxsize=None)
def band_tables():
    order = bin_order()
    nearby = np.abs(order[:, None] - order[None, :]) <= SMOOTH
    counts = nearby.sum(axis=0).astype(np.float32)
    return order.astype(np.float32), (1.0 / counts)[None, :].astype(np.float32)


@functools.lru_cache(maxsize=None)
def lag_table():
    freqs = FIRST_BIN + bin_order()
    phase = phases(freqs, np.arange(LAGS) - MAXLAG)
    return np.concatenate([np.cos(phase), -np.sin(phase)], axis=0).astype(ml_dtypes.bfloat16)


def pack_kernel(lengths_ref, start_ref, x_ref, out_ref):
    windows, channels, samples = x_ref.shape
    windows = windows // 2
    half = channels // 2
    sample = start_ref[0] + lax.broadcasted_iota(jnp.int32, (16, samples), 1)
    for core, w in itertools.product(range(2), range(windows)):
        inside = (sample < lengths_ref[core * windows + w]).astype(F32).astype(BF16)
        inside = jnp.concatenate([inside] * (half // 16), axis=0)
        for h in range(2):
            rows = slice(h * half, (h + 1) * half)
            out_ref[core, h, w] = x_ref[core * windows + w, rows, :] * inside


def pack(strain, lengths, start, chips):
    windows, channels, samples = strain.shape
    per_core = windows // 2
    chip_channels = channels // chips
    return pl.pallas_call(
        pack_kernel,
        grid=(chips,),
        in_specs=[
            pl.BlockSpec(memory_space=pltpu.SMEM),
            pl.BlockSpec(memory_space=pltpu.SMEM),
            pl.BlockSpec((windows, chip_channels, samples), lambda i: (0, i, 0)),
        ],
        out_specs=pl.BlockSpec(
            (2, 2, per_core, chip_channels // 2, samples), lambda i: (i, 0, 0, 0, 0)
        ),
        out_shape=jax.ShapeDtypeStruct(
            (2 * chips, 2, per_core, chip_channels // 2, samples), BF16
        ),
        compiler_params=pltpu.CompilerParams(vmem_limit_bytes=VMEM_LIMIT),
        name="pack",
    )(lengths, start, strain)


def transform_kernel(layout, core_ref, x_ref, table_hbm, sign_ref, bin_row_ref, bin_column_ref,
                     inverse_ref, select_ref,
                     own_hbm, other_hbm, *rest):
    send_refs = rest[:CLASSES]
    parts, real, imag, white_ref, table_ref, nearby_ref, sems = rest[CLASSES:]
    tiles = [(used[0][2], used[-1][2] + 1) for _, _, used in layout]
    copies = [
        pltpu.make_async_copy(table_hbm.at[a:b], table_ref.at[a:b], sems.at[i])
        for i, (a, b) in enumerate(tiles)
    ]
    for copy in copies:
        copy.start()
    slabs, rows, samples = x_ref.shape
    merge = PART // samples
    root = math.sqrt(0.5)
    step = 32

    def fold(i, carry):
        at = pl.ds(pl.multiple_of(i * step, step), step)
        x = []
        for a in range(RADIX):
            pieces = [x_ref[a * merge + j, at, :] for j in range(merge)]
            joined = pieces[0] if merge == 1 else jnp.concatenate(pieces, axis=-1)
            x.append(joined.astype(F32))
        s = [x[a] + x[a + 4] for a in range(4)]
        d = [x[a] - x[a + 4] for a in range(4)]
        even, odd = s[0] + s[2], s[1] + s[3]
        minus, plus = (d[1] - d[3]) * root, (d[1] + d[3]) * root
        values = (
            even + odd, even - odd, s[0] - s[2], s[3] - s[1],
            d[0] + minus, -(d[2] + plus), d[0] - minus, d[2] - plus,
        )
        for index, value in enumerate(values):
            parts[index, at, :] = value.astype(BF16)
        return carry

    for begin in range(0, NF, 128):
        gap = jnp.abs(bin_column_ref[begin : begin + 128, :] - bin_row_ref[...])
        nearby_ref[begin : begin + 128, :] = jnp.where(gap <= SMOOTH, 1.0, 0.0).astype(BF16)
    lax.fori_loop(0, rows // step, fold, 0)
    for copy, (begin, end, used) in zip(copies, layout):
        copy.wait()
        straight = crossed = None
        for real_part, imag_part, block in used:
            term = jnp.dot(parts[real_part], table_ref[block], preferred_element_type=F32)
            straight = term if straight is None else straight + term
            if imag_part is None:
                continue
            term = jnp.dot(parts[imag_part], table_ref[block], preferred_element_type=F32)
            crossed = term if crossed is None else crossed + term
        width = end - begin
        re, im = straight[:, :width], -straight[:, TILE : TILE + width]
        if crossed is not None:
            side = sign_ref[:, begin:end]
            re = re + crossed[:, TILE : TILE + width] * side
            im = im + crossed[:, :width] * side
        real[:, begin:end] = re
        imag[:, begin:end] = im
    re, im = real[...], imag[...]
    magnitude = jnp.sqrt(re * re + im * im).astype(BF16)
    smooth = jnp.dot(magnitude, nearby_ref[...], preferred_element_type=F32)
    inverse = 1.0 / (smooth * inverse_ref[...] + 1e-06)
    white_ref[:, :NF] = (real[...] * inverse).astype(BF16)
    white_ref[:, NF:] = (imag[...] * inverse).astype(BF16)
    half = rows // 2
    core = core_ref[0]
    halves = [
        pltpu.make_async_copy(
            white_ref.at[pl.ds(pl.multiple_of(side * half, half), half), :],
            ref,
            sems.at[len(copies) + i],
        )
        for i, (side, ref) in enumerate(((core, own_hbm), (1 - core, other_hbm)))
    ]
    for copy in halves:
        copy.start()
    lanes = send_refs[0].shape[1]
    for q, send_ref in enumerate(send_refs):
        chosen = jnp.dot(
            select_ref[q * lanes : (q + 1) * lanes, :], white_ref[...], preferred_element_type=F32
        )
        for begin in range(0, 2 * NF, 128):
            send_ref[begin : begin + 128, :] = jnp.transpose(
                chosen[:, begin : begin + 128]
            ).astype(BF16)
    for copy in halves:
        copy.wait()


def transform(received, select, core, lanes):
    slabs, rows, samples = received.shape
    table, sign, layout = forward_blocks()
    bins, inverse = band_tables()
    whole = pl.BlockSpec(memory_space=pltpu.VMEM)
    return pl.pallas_call(
        functools.partial(transform_kernel, layout),
        in_specs=[pl.BlockSpec(memory_space=pltpu.SMEM), whole]
        + [pl.BlockSpec(memory_space=pl.ANY)]
        + [whole] * 5,
        out_specs=[pl.BlockSpec(memory_space=pl.ANY)] * 2 + [whole] * CLASSES,
        out_shape=[
            jax.ShapeDtypeStruct((rows // 2, 2 * NF), BF16),
            jax.ShapeDtypeStruct((rows // 2, 2 * NF), BF16),
        ]
        + [jax.ShapeDtypeStruct((2 * NF, lanes), BF16)] * CLASSES,
        scratch_shapes=[
            pltpu.VMEM((RADIX, rows, PART), BF16),
            pltpu.VMEM((rows, NF), F32),
            pltpu.VMEM((rows, NF), F32),
            pltpu.VMEM((rows, 2 * NF), BF16),
            pltpu.VMEM(table.shape, BF16),
            pltpu.VMEM((NF, NF), BF16),
            pltpu.SemaphoreType.DMA((len(layout) + 2,)),
        ],
        compiler_params=pltpu.CompilerParams(vmem_limit_bytes=VMEM_LIMIT),
        name="transform",
    )(core, received, table, sign, bins[None, :], bins[:, None], inverse, select)


def gather_bins_kernel(mine_ref, theirs_ref, out_ref):
    windows, channels, _ = mine_ref.shape
    lane = lax.broadcasted_iota(jnp.int32, (channels, 128), 1)
    odd = lax.broadcasted_iota(jnp.int32, (channels, 128), 0) % 2 == 1
    upper = [((lane // (8 << bit)) % 2) == 1 for bit in range(4)]

    def turned(tiles):
        tiles = list(tiles)
        for bit in range(4):
            shift = 8 << bit
            for j in range(16):
                if (j >> bit) & 1:
                    continue
                low, high = tiles[j], tiles[j + (1 << bit)]
                if low is None and high is None:
                    continue
                zero = jnp.zeros((channels, 128), F32)
                low = zero if low is None else low
                high = zero if high is None else high
                tiles[j] = jnp.where(upper[bit], pltpu.roll(high, shift, 1), low)
                tiles[j + (1 << bit)] = jnp.where(
                    upper[bit], high, pltpu.roll(low, 128 - shift, 1)
                )
        return tiles

    def tile(i, carry):
        at = pl.ds(pl.multiple_of(i * 128, 128), 128)
        at_im = pl.ds(pl.multiple_of(NF + i * 128, 128), 128)
        first_half, second_half = [], []
        for ref in (mine_ref, theirs_ref):
            for w in range(windows):
                re, im = ref[w, :, at].astype(F32), ref[w, :, at_im].astype(F32)
                first_half.append(jnp.where(odd, -im, re))
                second_half.append(jnp.where(odd, re, im))
        values = first_half + second_half
        first = turned(values[:16])
        second = turned(values[16:] + [None] * (32 - len(values)))
        for g in range(16):
            out_ref[i * 16 + g, :, :128] = first[g]
            out_ref[i * 16 + g, :, 128:] = second[g]
        return carry

    lax.fori_loop(0, NF // 128, tile, 0)


def gather_bins(mine, theirs):
    windows, channels, _ = mine.shape
    whole = pl.BlockSpec(memory_space=pltpu.VMEM)
    return pl.pallas_call(
        gather_bins_kernel,
        in_specs=[whole] * 2,
        out_specs=whole,
        out_shape=jax.ShapeDtypeStruct((NF // 8, channels, TILE), F32),
        compiler_params=pltpu.CompilerParams(vmem_limit_bytes=VMEM_LIMIT),
        name="gather_bins",
    )(mine, theirs)


def correlate_kernel(segs, mine_hbm, theirs_hbm, own_hbm, table_hbm, place_ref, order_ref,
                     out_ref, src, cross, mine_ref, theirs_ref, own_ref, table_ref, sems):
    copies = [
        pltpu.make_async_copy(a, b, sems.at[i])
        for i, (a, b) in enumerate(
            (
                (mine_hbm, mine_ref),
                (theirs_hbm, theirs_ref),
                (own_hbm, own_ref),
                (table_hbm, table_ref),
            )
        )
    ]
    for copy in copies:
        copy.start()
    channels = own_ref.shape[1]
    sources = 64
    windows = place_ref.shape[1] // sources
    low = lax.broadcasted_iota(jnp.int32, (NF, 128), 1) < sources

    def spread(part, values, places):
        for begin in range(0, windows * sources, TILE):
            at = places[:, begin : begin + TILE]
            re = jnp.dot(values[:NF], at, preferred_element_type=F32)
            im = jnp.dot(values[NF:], at, preferred_element_type=F32)
            for near in range(0, at.shape[1], 128):
                r, i = re[:, near : near + 128], im[:, near : near + 128]
                turned_r, turned_i = pltpu.roll(r, sources, 1), pltpu.roll(i, sources, 1)
                first = part * windows + (begin + near) // sources
                src[first] = jnp.where(low, r, -turned_i)
                src[first + 1] = jnp.where(low, turned_r, -i)
                second = first + 2 * windows
                src[second] = jnp.where(low, i, turned_r)
                src[second + 1] = jnp.where(low, turned_i, r)

    for part, ref in enumerate((mine_ref, theirs_ref)):
        copies[part].wait()
        joined = jnp.concatenate([ref[d] for d in range(ref.shape[0])], axis=1)
        spread(part, joined, place_ref)

    shape = (8, TILE)
    lane = lax.broadcasted_iota(jnp.int32, shape, 1)
    place = lax.broadcasted_iota(jnp.int32, shape, 0)
    pick = (lane % 4 == place % 4) & (lane < 32 * windows)
    upper = place < 4
    early = lax.broadcasted_iota(jnp.int32, (8, 128), 0) < 4
    under = lax.broadcasted_iota(jnp.int32, (16, 128), 1) < sources
    zeros = jnp.zeros((TILE - 32 * windows, TILE), F32)

    def bins(i, carry):
        pair = []
        for e in range(2):
            g = 2 * i + e
            at = pl.ds(pl.multiple_of(g * 8, 8), 8)
            right = []
            for j in range(4 * windows):
                tile = src[j, at, :]
                halves = [jnp.where(early, tile, 0.0), jnp.where(early, 0.0, tile)]
                right.append(jnp.concatenate(halves, axis=1))
            right = jnp.concatenate(right + [zeros], axis=0).astype(BF16)
            left = []
            for c in range(0, channels, 2):
                even = jnp.broadcast_to(own_ref[g, c : c + 1, :], shape)
                uneven = jnp.broadcast_to(own_ref[g, c + 1 : c + 2, :], shape)
                left.append(jnp.where(pick, jnp.where(upper, even, uneven), 0.0))
            left = jnp.concatenate(left, axis=0).astype(BF16)
            pair.append(jnp.dot(left, right, preferred_element_type=F32))
        at = pl.ds(pl.multiple_of(i * 16, 16), 16)
        at_im = pl.ds(pl.multiple_of(NF + i * 16, 16), 16)
        for c in range(0, channels, 2):
            t = [[], []]
            for p in pair:
                first, last = p[c * 4 : c * 4 + 8, :128], p[c * 4 : c * 4 + 8, 128:]
                t[0].append(jnp.where(early, first, pltpu.roll(last, 4, 0)))
                t[1].append(jnp.where(early, pltpu.roll(first, 4, 0), last))
            t = [jnp.concatenate(tiles, axis=0) for tiles in t]
            re = jnp.where(under, t[0], t[1])
            im = pltpu.roll(jnp.where(under, -t[1], t[0]), sources, 1)
            lanes = slice((c % 4) * 64, (c % 4) * 64 + 128)
            cross[c // 4, at, lanes] = re.astype(BF16)
            cross[c // 4, at_im, lanes] = im.astype(BF16)
        return carry

    copies[2].wait()
    lax.fori_loop(0, NF // 16, bins, 0, unroll=8)

    rows = TILE // segs

    def lags(i, carry):
        lag = jnp.concatenate(
            [
                jnp.dot(
                    table_ref[n : n + TILE, :], cross[i], preferred_element_type=F32
                ).astype(BF16)
                for n in range(0, LAGS, TILE)
            ],
            axis=0,
        )
        turned = lax.dot_general(
            order_ref[...], lag, (((1,), (1,)), ((), ())), preferred_element_type=F32
        ).astype(BF16)
        at = pl.ds(pl.multiple_of(i * rows, rows), rows)
        for g in range(segs):
            out_ref[g, at, :] = turned[g * rows : (g + 1) * rows, :]
        return carry

    copies[3].wait()
    lax.fori_loop(0, channels // 4, lags, 0)


def correlate(own, mine, theirs, place, segs):
    groups, channels, _ = own.shape
    windows = place.shape[1] // 64
    group = 64 // segs
    order = np.zeros((segs, 4, group, 4, segs, group), np.float32)
    for g, c, u in itertools.product(range(segs), range(4), range(group)):
        order[g, c, u, c, g, u] = 1
    order = order.reshape(256, 256).astype(ml_dtypes.bfloat16)
    table = np.ascontiguousarray(lag_table().T)
    whole = pl.BlockSpec(memory_space=pltpu.VMEM)
    return pl.pallas_call(
        functools.partial(correlate_kernel, segs),
        in_specs=[pl.BlockSpec(memory_space=pl.ANY)] * 4 + [whole] * 2,
        out_specs=whole,
        out_shape=jax.ShapeDtypeStruct((segs, channels * group, LAGS), BF16),
        scratch_shapes=[
            pltpu.VMEM((4 * windows, NF, 128), F32),
            pltpu.VMEM((channels // 4, 2 * NF, TILE), BF16),
            pltpu.VMEM(mine.shape, BF16),
            pltpu.VMEM(theirs.shape, BF16),
            pltpu.VMEM(own.shape, F32),
            pltpu.VMEM(table.shape, BF16),
            pltpu.SemaphoreType.DMA((4,)),
        ],
        compiler_params=pltpu.CompilerParams(vmem_limit_bytes=VMEM_LIMIT),
        name="correlate",
    )(mine, theirs, own, table, place, order)


def finish_kernel(scale, place_ref, *refs):
    parts, out_ref = refs[:-1], refs[-1]
    segs = parts[0].shape[0]
    pairs = out_ref.shape[0] // 2
    rows = parts[0].shape[1] // pairs
    block = out_ref.shape[1]
    for i in range(pairs):
        stacked = jnp.concatenate(
            [part[g, i * rows : (i + 1) * rows, :] for g in range(segs) for part in parts], axis=0
        )
        total = jnp.dot(place_ref[...], stacked, preferred_element_type=F32) * scale
        out_ref[2 * i : 2 * i + 2] = total.reshape(2, block, LAGS)


def finish(parts, place, scale, block, channels):
    segs, rows, _ = parts[0].shape
    step = math.gcd(channels, 16)
    piece = pl.BlockSpec((segs, rows * step // channels, LAGS), lambda i: (0, i, 0))
    return pl.pallas_call(
        functools.partial(finish_kernel, scale),
        grid=(channels // step,),
        in_specs=[pl.BlockSpec(place.shape, lambda i: (0, 0))] + [piece] * len(parts),
        out_specs=pl.BlockSpec((step, block, LAGS), lambda i: (i, 0, 0)),
        out_shape=jax.ShapeDtypeStruct((channels, block, LAGS), F32),
        compiler_params=pltpu.CompilerParams(vmem_limit_bytes=VMEM_LIMIT),
        name="finish",
    )(place, *parts)


def round_up(value, step):
    return -(-value // step) * step


def plan(source_channel, chips, chip_channels, segs):
    count = source_channel.shape[0]
    block = count // segs
    chip = source_channel // chip_channels
    index = jnp.arange(count, dtype=jnp.int32)
    seg = index // block
    same_seg = seg[:, None] == seg[None, :]
    earlier = index[None, :] < index[:, None]
    same_chip = chip[:, None] == chip[None, :]
    ahead = same_seg & ((chip[None, :] < chip[:, None]) | (same_chip & earlier))
    position = jnp.sum(ahead.astype(jnp.int32), axis=1)
    turns = np.array(
        [(0,) + t for t in itertools.product(range(CLASSES), repeat=segs - 1)], np.int32
    )
    turned = jnp.asarray(np.repeat(turns, block, axis=1))
    classes = (position[None, :] + turned) % CLASSES
    of_class = classes[:, None, :] == jnp.arange(CLASSES, dtype=jnp.int32)[None, :, None]
    of_chip = chip[:, None] == jnp.arange(chips, dtype=jnp.int32)[None, :]
    held = jnp.einsum(
        "rqs,sz->rqz", of_class.astype(BF16), of_chip.astype(BF16), preferred_element_type=F32
    )
    fullest = jnp.max(held, axis=(1, 2))
    best = jnp.argmin(fullest)
    chosen = lax.dynamic_index_in_dim(classes, best, 0, keepdims=False)
    same_class = chosen[:, None] == chosen[None, :]
    place = jnp.sum(
        (same_seg & same_class & (position[None, :] < position[:, None])).astype(jnp.int32), axis=1
    )
    slot = jnp.sum((same_chip & same_class & earlier).astype(jnp.int32), axis=1)
    return chip, chosen, place, slot, seg, jnp.min(fullest)


def on_device(strain_rate, window_length, source_channel):
    chan_index = lax.axis_index("chan")
    seg_index = lax.axis_index("seg")
    devices = lax.axis_size("chan")
    segs = lax.axis_size("seg")
    chips = devices // 2
    windows, all_channels, samples = strain_rate.shape
    channels = all_channels // devices
    per_core = windows // 2
    count = source_channel.shape[0]
    block = count // segs
    group = block // CLASSES
    spots = segs * group
    my_chip = chan_index // 2
    my_core = (chan_index % 2).astype(jnp.int32).reshape(1)

    start = (chan_index * samples).astype(jnp.int32).reshape(1)
    packed = pack(strain_rate, window_length, start, chips)
    packed = packed.reshape(devices, 2 * per_core * channels, samples)
    received = lax.all_to_all(packed, "chan", split_axis=0, concat_axis=0, tiled=True)

    chip, chosen, place, slot, seg, fullest = plan(source_channel, chips, 2 * channels, segs)
    lanes = round_up(per_core * -(-count // (CLASSES * chips)), 128)
    cap = lanes // per_core
    full = (fullest > cap).astype(jnp.int32)

    core_swap = [(i, i ^ 1) for i in range(devices)]
    upward = [(i, i + 2) for i in range(devices - 2)]
    downward = [(i + 2, i) for i in range(devices - 2)]
    lines = [list(range(core, devices, 2)) for core in range(2)]

    row = np.arange(2 * per_core * channels)
    row_window = (row // channels) % per_core
    row_channel = (row // (per_core * channels)) * channels + row % channels
    kinds = jnp.arange(CLASSES, dtype=jnp.int32)
    local = source_channel % (2 * channels)
    here = chip == my_chip

    seat = np.arange(lanes)
    seat_window = np.where(seat < per_core * cap, seat // cap, -1).astype(np.int32)
    seat_slot = (seat % cap).astype(np.int32)
    sits = (
        (chosen[None, None, :] == kinds[:, None, None])
        & (slot[None, None, :] == seat_slot[None, :, None])
        & here[None, None, :]
    )
    held = jnp.sum(jnp.where(sits, local[None, None, :] + 1, 0), axis=-1) - 1
    select = (
        (held[:, :, None] == row_channel[None, None, :])
        & (seat_window[:, None] == row_window[None, :])[None]
    ).astype(BF16).reshape(CLASSES * lanes, row.shape[0])

    spot_index = jnp.arange(spots, dtype=jnp.int32)
    at_spot = (
        (chosen[None, None, :] == kinds[:, None, None])
        & (seg * group + place == spot_index[:, None])[None]
    )
    spot_slot = jnp.sum(jnp.where(at_spot, slot[None, None, :], 0), axis=-1)
    spot_chip = jnp.sum(jnp.where(at_spot, chip[None, None, :], 0), axis=-1)
    spot_far = jnp.stack([(spot_chip[0] - my_chip) % chips, spot_chip[1]])
    column_window = np.repeat(np.arange(per_core), spots)
    far = np.repeat(np.arange(chips), lanes).astype(np.int32)
    placing = (
        (jnp.tile(spot_slot, (1, per_core))[:, None, :] == np.tile(seat_slot, chips)[None, :, None])
        & (jnp.tile(spot_far, (1, per_core))[:, None, :] == far[None, :, None])
        & (np.tile(seat_window, chips)[:, None] == column_window[None, :])[None]
    ).astype(BF16)

    my_chosen = lax.dynamic_slice_in_dim(chosen, seg_index * block, block)
    my_place = lax.dynamic_slice_in_dim(place, seg_index * block, block)
    width = CLASSES * 2 * group
    column = np.arange(segs * width) % width
    row_pair = np.repeat(np.arange(2), block)
    final = (
        (jnp.tile(my_chosen, 2)[:, None] == (column // (2 * group))[None, :])
        & (jnp.tile(my_place, 2)[:, None] == (column % group)[None, :])
        & (row_pair[:, None] == (column // group % 2)[None, :])
    ).astype(BF16)

    own, other, *sends = transform(received, select, my_core, lanes)
    own_other = lax.ppermute(other, "chan", core_swap)
    shape = (per_core, channels, 2 * NF)
    bins = gather_bins(own.reshape(shape), own_other.reshape(shape))

    from_below, from_above = [None] * chips, [None] * chips
    up = down = sends[0]
    for hop in range(1, chips):
        up = lax.ppermute(up, "chan", upward)
        down = lax.ppermute(down, "chan", downward)
        if hop == 2:
            up, down, bins, second = lax.optimization_barrier((up, down, bins, sends[1]))
        from_below[hop], from_above[hop] = up, down
    second = lax.all_gather(second, "chan", axis_index_groups=lines)
    merged = [sends[0]]
    for far_by in range(1, chips):
        merged.append(from_above[far_by] + from_below[chips - far_by])

    def stacks(mine, places):
        theirs = lax.ppermute(mine, "chan", core_swap)
        return correlate(bins, mine, theirs, places, segs)

    scale = 1.0 / math.sqrt(NF * windows * segs)

    def finished(lags):
        pieces = [
            lax.all_to_all(lag, "seg", split_axis=0, concat_axis=0, tiled=True) for lag in lags
        ]
        return finish(pieces, final, scale, block, channels)

    first_lag = stacks(jnp.stack(merged), placing[0])
    first_lag, second = lax.optimization_barrier((first_lag, second))
    second_lag = stacks(second, placing[1])
    seated = finished([first_lag, second_lag])

    def add_unseated(turn, total):
        out = (slot >= cap) & (turn < full)
        at = jnp.sum(jnp.where(at_spot & here & out, local[None, None, :] + 1, 0), axis=-1) - 1
        wanted = (
            (jnp.tile(at, (1, per_core))[:, :, None] == row_channel[None, None, :])
            & (np.repeat(np.arange(per_core), spots)[:, None] == row_window[None, :])[None]
        ).astype(BF16)
        spot = jnp.eye(per_core * spots, dtype=BF16)
        first = my_core[0] == 0
        white = jnp.concatenate([jnp.where(first, own, other), jnp.where(first, other, own)])
        lags = []
        for q in range(CLASSES):
            mine = jnp.einsum("sr,rk->ks", wanted[q], white, preferred_element_type=F32)
            mine = lax.psum(mine.astype(BF16), "chan", axis_index_groups=lines)
            lags.append(stacks(mine[None], spot))
        return total + finished(lags)

    _, stacked = lax.while_loop(
        lambda carry: carry[0] < full,
        lambda carry: (carry[0] + 1, add_unseated(*carry)),
        (jnp.zeros((), jnp.int32), seated),
    )
    return stacked


def solution(mesh):
    in_specs = (P("seg", None, "chan"), P("seg"), P())
    out_specs = P("chan", "seg", None)
    return jax.shard_map(
        on_device, mesh=mesh, in_specs=in_specs, out_specs=out_specs, check_vma=False
    )
```

```python
import functools
import itertools
import math

import jax
import jax.numpy as jnp
import ml_dtypes
import numpy as np
from jax import lax
from jax.experimental import pallas as pl
from jax.experimental.pallas import tpu as pltpu
from jax.sharding import PartitionSpec as P

W = 4096
NF = 1152
FIRST_BIN = 16
SMOOTH = 64
MAXLAG = 256
LAGS = 512
RADIX = 8
PART = W // RADIX
TILE = 256
CLASSES = 2
BF16 = jnp.bfloat16
F32 = jnp.float32
VMEM_LIMIT = 60 * 1024 * 1024
GROUPS = ((0,), (4,), (2, 6), (1, 7), (3, 5))
COMPONENTS = {0: (0, None), 4: (1, None), 2: (2, 3), 1: (4, 5), 3: (6, 7)}


def phases(first, second):
    product = np.mod(first[:, None].astype(np.int64) * second[None, :], W)
    return product.astype(np.float32) * np.float32(2.0 * math.pi / W)


@functools.lru_cache(maxsize=None)
def bin_order():
    residue = (FIRST_BIN + np.arange(NF)) % RADIX
    return np.concatenate([np.nonzero(residue == r)[0] for group in GROUPS for r in group])


@functools.lru_cache(maxsize=None)
def forward_blocks():
    order = bin_order()
    freqs = FIRST_BIN + order
    residue = freqs % RADIX
    phase = phases(np.arange(PART), freqs)
    cos, sin = np.cos(phase), np.sin(phase)
    base = np.minimum(residue, RADIX - residue)
    sign = np.where(residue == base, 1.0, -1.0).astype(np.float32)
    blocks, layout = [], []
    for begin in range(0, NF, TILE):
        end = min(begin + TILE, NF)
        used = []
        for root, (real_part, imag_part) in COMPONENTS.items():
            hit = (base[begin:end] == root).astype(np.float32)
            if not hit.any():
                continue
            block = np.zeros((PART, 2 * TILE), np.float32)
            block[:, : end - begin] = cos[:, begin:end] * hit
            block[:, TILE : TILE + end - begin] = sin[:, begin:end] * hit
            used.append((real_part, imag_part, len(blocks)))
            blocks.append(block)
        layout.append((begin, end, used))
    return np.stack(blocks).astype(ml_dtypes.bfloat16), sign[None, :], layout


@functools.lru_cache(maxsize=None)
def band_tables():
    order = bin_order()
    nearby = np.abs(order[:, None] - order[None, :]) <= SMOOTH
    counts = nearby.sum(axis=0).astype(np.float32)
    return order.astype(np.float32), (1.0 / counts)[None, :].astype(np.float32)


@functools.lru_cache(maxsize=None)
def lag_table():
    freqs = FIRST_BIN + bin_order()
    phase = phases(freqs, np.arange(LAGS) - MAXLAG)
    return np.concatenate([np.cos(phase), -np.sin(phase)], axis=0).astype(ml_dtypes.bfloat16)


def pack_kernel(lengths_ref, start_ref, x_ref, out_ref):
    windows, channels, samples = x_ref.shape
    windows = windows // 2
    half = channels // 2
    sample = start_ref[0] + lax.broadcasted_iota(jnp.int32, (16, samples), 1)
    for core, w in itertools.product(range(2), range(windows)):
        inside = (sample < lengths_ref[core * windows + w]).astype(F32).astype(BF16)
        inside = jnp.concatenate([inside] * (half // 16), axis=0)
        for h in range(2):
            rows = slice(h * half, (h + 1) * half)
            out_ref[core, h, w] = x_ref[core * windows + w, rows, :] * inside


def pack(strain, lengths, start, chips):
    windows, channels, samples = strain.shape
    per_core = windows // 2
    chip_channels = channels // chips
    return pl.pallas_call(
        pack_kernel,
        grid=(chips,),
        in_specs=[
            pl.BlockSpec(memory_space=pltpu.SMEM),
            pl.BlockSpec(memory_space=pltpu.SMEM),
            pl.BlockSpec((windows, chip_channels, samples), lambda i: (0, i, 0)),
        ],
        out_specs=pl.BlockSpec(
            (2, 2, per_core, chip_channels // 2, samples), lambda i: (i, 0, 0, 0, 0)
        ),
        out_shape=jax.ShapeDtypeStruct(
            (2 * chips, 2, per_core, chip_channels // 2, samples), BF16
        ),
        compiler_params=pltpu.CompilerParams(vmem_limit_bytes=VMEM_LIMIT),
        name="pack",
    )(lengths, start, strain)


def transform_kernel(layout, core_ref, x_ref, table_hbm, sign_ref, bin_row_ref, bin_column_ref,
                     inverse_ref, select_ref,
                     own_ref, other_ref, *rest):
    send_refs = rest[:CLASSES]
    parts, real, imag, white_ref, table_ref, nearby_ref, sems = rest[CLASSES:]
    tiles = [(used[0][2], used[-1][2] + 1) for _, _, used in layout]
    copies = [
        pltpu.make_async_copy(table_hbm.at[a:b], table_ref.at[a:b], sems.at[i])
        for i, (a, b) in enumerate(tiles)
    ]
    for copy in copies:
        copy.start()
    slabs, rows, samples = x_ref.shape
    merge = PART // samples
    root = math.sqrt(0.5)
    step = 32

    def fold(i, carry):
        at = pl.ds(pl.multiple_of(i * step, step), step)
        x = []
        for a in range(RADIX):
            pieces = [x_ref[a * merge + j, at, :] for j in range(merge)]
            joined = pieces[0] if merge == 1 else jnp.concatenate(pieces, axis=-1)
            x.append(joined.astype(F32))
        s = [x[a] + x[a + 4] for a in range(4)]
        d = [x[a] - x[a + 4] for a in range(4)]
        even, odd = s[0] + s[2], s[1] + s[3]
        minus, plus = (d[1] - d[3]) * root, (d[1] + d[3]) * root
        values = (
            even + odd, even - odd, s[0] - s[2], s[3] - s[1],
            d[0] + minus, -(d[2] + plus), d[0] - minus, d[2] - plus,
        )
        for index, value in enumerate(values):
            parts[index, at, :] = value.astype(BF16)
        return carry

    for begin in range(0, NF, 128):
        gap = jnp.abs(bin_column_ref[begin : begin + 128, :] - bin_row_ref[...])
        nearby_ref[begin : begin + 128, :] = jnp.where(gap <= SMOOTH, 1.0, 0.0).astype(BF16)
    lax.fori_loop(0, rows // step, fold, 0)
    for copy, (begin, end, used) in zip(copies, layout):
        copy.wait()
        straight = crossed = None
        for real_part, imag_part, block in used:
            term = jnp.dot(parts[real_part], table_ref[block], preferred_element_type=F32)
            straight = term if straight is None else straight + term
            if imag_part is None:
                continue
            term = jnp.dot(parts[imag_part], table_ref[block], preferred_element_type=F32)
            crossed = term if crossed is None else crossed + term
        width = end - begin
        re, im = straight[:, :width], -straight[:, TILE : TILE + width]
        if crossed is not None:
            side = sign_ref[:, begin:end]
            re = re + crossed[:, TILE : TILE + width] * side
            im = im + crossed[:, :width] * side
        real[:, begin:end] = re
        imag[:, begin:end] = im
    re, im = real[...], imag[...]
    magnitude = jnp.sqrt(re * re + im * im).astype(BF16)
    smooth = jnp.dot(magnitude, nearby_ref[...], preferred_element_type=F32)
    inverse = 1.0 / (smooth * inverse_ref[...] + 1e-06)
    white_ref[:, :NF] = (real[...] * inverse).astype(BF16)
    white_ref[:, NF:] = (imag[...] * inverse).astype(BF16)
    half = rows // 2
    core = core_ref[0]
    own_ref[...] = white_ref[pl.ds(pl.multiple_of(core * half, half), half), :]
    other_ref[...] = white_ref[pl.ds(pl.multiple_of((1 - core) * half, half), half), :]
    lanes = send_refs[0].shape[1]
    for q, send_ref in enumerate(send_refs):
        chosen = jnp.dot(
            select_ref[q * lanes : (q + 1) * lanes, :], white_ref[...], preferred_element_type=F32
        )
        for begin in range(0, 2 * NF, 128):
            send_ref[begin : begin + 128, :] = jnp.transpose(
                chosen[:, begin : begin + 128]
            ).astype(BF16)


def transform(received, select, core, lanes):
    slabs, rows, samples = received.shape
    table, sign, layout = forward_blocks()
    bins, inverse = band_tables()
    whole = pl.BlockSpec(memory_space=pltpu.VMEM)
    return pl.pallas_call(
        functools.partial(transform_kernel, layout),
        in_specs=[pl.BlockSpec(memory_space=pltpu.SMEM), whole]
        + [pl.BlockSpec(memory_space=pl.ANY)]
        + [whole] * 5,
        out_specs=[whole] * (2 + CLASSES),
        out_shape=[
            jax.ShapeDtypeStruct((rows // 2, 2 * NF), BF16),
            jax.ShapeDtypeStruct((rows // 2, 2 * NF), BF16),
        ]
        + [jax.ShapeDtypeStruct((2 * NF, lanes), BF16)] * CLASSES,
        scratch_shapes=[
            pltpu.VMEM((RADIX, rows, PART), BF16),
            pltpu.VMEM((rows, NF), F32),
            pltpu.VMEM((rows, NF), F32),
            pltpu.VMEM((rows, 2 * NF), BF16),
            pltpu.VMEM(table.shape, BF16),
            pltpu.VMEM((NF, NF), BF16),
            pltpu.SemaphoreType.DMA((len(layout),)),
        ],
        compiler_params=pltpu.CompilerParams(vmem_limit_bytes=VMEM_LIMIT),
        name="transform",
    )(core, received, table, sign, bins[None, :], bins[:, None], inverse, select)


def gather_bins_kernel(mine_ref, theirs_ref, out_ref):
    windows, channels, _ = mine_ref.shape
    lane = lax.broadcasted_iota(jnp.int32, (channels, 128), 1)
    odd = lax.broadcasted_iota(jnp.int32, (channels, 128), 0) % 2 == 1
    upper = [((lane // (8 << bit)) % 2) == 1 for bit in range(4)]

    def turned(tiles):
        tiles = list(tiles)
        for bit in range(4):
            shift = 8 << bit
            for j in range(16):
                if (j >> bit) & 1:
                    continue
                low, high = tiles[j], tiles[j + (1 << bit)]
                if low is None and high is None:
                    continue
                zero = jnp.zeros((channels, 128), F32)
                low = zero if low is None else low
                high = zero if high is None else high
                tiles[j] = jnp.where(upper[bit], pltpu.roll(high, shift, 1), low)
                tiles[j + (1 << bit)] = jnp.where(
                    upper[bit], high, pltpu.roll(low, 128 - shift, 1)
                )
        return tiles

    def tile(i, carry):
        at = pl.ds(pl.multiple_of(i * 128, 128), 128)
        at_im = pl.ds(pl.multiple_of(NF + i * 128, 128), 128)
        first_half, second_half = [], []
        for ref in (mine_ref, theirs_ref):
            for w in range(windows):
                re, im = ref[w, :, at].astype(F32), ref[w, :, at_im].astype(F32)
                first_half.append(jnp.where(odd, -im, re))
                second_half.append(jnp.where(odd, re, im))
        values = first_half + second_half
        first = turned(values[:16])
        second = turned(values[16:] + [None] * (32 - len(values)))
        for g in range(16):
            out_ref[i * 16 + g, :, :128] = first[g]
            out_ref[i * 16 + g, :, 128:] = second[g]
        return carry

    lax.fori_loop(0, NF // 128, tile, 0)


def gather_bins(mine, theirs):
    windows, channels, _ = mine.shape
    whole = pl.BlockSpec(memory_space=pltpu.VMEM)
    return pl.pallas_call(
        gather_bins_kernel,
        in_specs=[whole] * 2,
        out_specs=whole,
        out_shape=jax.ShapeDtypeStruct((NF // 8, channels, TILE), F32),
        compiler_params=pltpu.CompilerParams(vmem_limit_bytes=VMEM_LIMIT),
        name="gather_bins",
    )(mine, theirs)


def correlate_kernel(segs, mine_hbm, theirs_hbm, own_hbm, table_hbm, place_ref, order_ref,
                     out_ref, src, cross, mine_ref, theirs_ref, own_ref, table_ref, sems):
    copies = [
        pltpu.make_async_copy(a, b, sems.at[i])
        for i, (a, b) in enumerate(
            (
                (mine_hbm, mine_ref),
                (theirs_hbm, theirs_ref),
                (own_hbm, own_ref),
                (table_hbm, table_ref),
            )
        )
    ]
    for copy in copies:
        copy.start()
    channels = own_ref.shape[1]
    sources = 64
    windows = place_ref.shape[1] // sources
    low = lax.broadcasted_iota(jnp.int32, (NF, 128), 1) < sources

    def spread(part, values, places):
        for begin in range(0, windows * sources, TILE):
            at = places[:, begin : begin + TILE]
            re = jnp.dot(values[:NF], at, preferred_element_type=F32)
            im = jnp.dot(values[NF:], at, preferred_element_type=F32)
            for near in range(0, at.shape[1], 128):
                r, i = re[:, near : near + 128], im[:, near : near + 128]
                turned_r, turned_i = pltpu.roll(r, sources, 1), pltpu.roll(i, sources, 1)
                first = part * windows + (begin + near) // sources
                src[first] = jnp.where(low, r, -turned_i)
                src[first + 1] = jnp.where(low, turned_r, -i)
                second = first + 2 * windows
                src[second] = jnp.where(low, i, turned_r)
                src[second + 1] = jnp.where(low, turned_i, r)

    for part, ref in enumerate((mine_ref, theirs_ref)):
        copies[part].wait()
        joined = jnp.concatenate([ref[d] for d in range(ref.shape[0])], axis=1)
        spread(part, joined, place_ref)

    shape = (8, TILE)
    lane = lax.broadcasted_iota(jnp.int32, shape, 1)
    place = lax.broadcasted_iota(jnp.int32, shape, 0)
    pick = (lane % 4 == place % 4) & (lane < 32 * windows)
    upper = place < 4
    early = lax.broadcasted_iota(jnp.int32, (8, 128), 0) < 4
    under = lax.broadcasted_iota(jnp.int32, (16, 128), 1) < sources
    zeros = jnp.zeros((TILE - 32 * windows, TILE), F32)

    def bins(i, carry):
        pair = []
        for e in range(2):
            g = 2 * i + e
            at = pl.ds(pl.multiple_of(g * 8, 8), 8)
            right = []
            for j in range(4 * windows):
                tile = src[j, at, :]
                halves = [jnp.where(early, tile, 0.0), jnp.where(early, 0.0, tile)]
                right.append(jnp.concatenate(halves, axis=1))
            right = jnp.concatenate(right + [zeros], axis=0).astype(BF16)
            left = []
            for c in range(0, channels, 2):
                even = jnp.broadcast_to(own_ref[g, c : c + 1, :], shape)
                uneven = jnp.broadcast_to(own_ref[g, c + 1 : c + 2, :], shape)
                left.append(jnp.where(pick, jnp.where(upper, even, uneven), 0.0))
            left = jnp.concatenate(left, axis=0).astype(BF16)
            pair.append(jnp.dot(left, right, preferred_element_type=F32))
        at = pl.ds(pl.multiple_of(i * 16, 16), 16)
        at_im = pl.ds(pl.multiple_of(NF + i * 16, 16), 16)
        for c in range(0, channels, 2):
            t = [[], []]
            for p in pair:
                first, last = p[c * 4 : c * 4 + 8, :128], p[c * 4 : c * 4 + 8, 128:]
                t[0].append(jnp.where(early, first, pltpu.roll(last, 4, 0)))
                t[1].append(jnp.where(early, pltpu.roll(first, 4, 0), last))
            t = [jnp.concatenate(tiles, axis=0) for tiles in t]
            re = jnp.where(under, t[0], t[1])
            im = pltpu.roll(jnp.where(under, -t[1], t[0]), sources, 1)
            lanes = slice((c % 4) * 64, (c % 4) * 64 + 128)
            cross[c // 4, at, lanes] = re.astype(BF16)
            cross[c // 4, at_im, lanes] = im.astype(BF16)
        return carry

    copies[2].wait()
    lax.fori_loop(0, NF // 16, bins, 0, unroll=8)

    rows = TILE // segs

    def lags(i, carry):
        lag = jnp.concatenate(
            [
                jnp.dot(
                    table_ref[n : n + TILE, :], cross[i], preferred_element_type=F32
                ).astype(BF16)
                for n in range(0, LAGS, TILE)
            ],
            axis=0,
        )
        turned = lax.dot_general(
            order_ref[...], lag, (((1,), (1,)), ((), ())), preferred_element_type=F32
        ).astype(BF16)
        at = pl.ds(pl.multiple_of(i * rows, rows), rows)
        for g in range(segs):
            out_ref[g, at, :] = turned[g * rows : (g + 1) * rows, :]
        return carry

    copies[3].wait()
    lax.fori_loop(0, channels // 4, lags, 0)


def correlate(own, mine, theirs, place, segs):
    groups, channels, _ = own.shape
    windows = place.shape[1] // 64
    group = 64 // segs
    order = np.zeros((segs, 4, group, 4, segs, group), np.float32)
    for g, c, u in itertools.product(range(segs), range(4), range(group)):
        order[g, c, u, c, g, u] = 1
    order = order.reshape(256, 256).astype(ml_dtypes.bfloat16)
    table = np.ascontiguousarray(lag_table().T)
    whole = pl.BlockSpec(memory_space=pltpu.VMEM)
    return pl.pallas_call(
        functools.partial(correlate_kernel, segs),
        in_specs=[pl.BlockSpec(memory_space=pl.ANY)] * 4 + [whole] * 2,
        out_specs=whole,
        out_shape=jax.ShapeDtypeStruct((segs, channels * group, LAGS), BF16),
        scratch_shapes=[
            pltpu.VMEM((4 * windows, NF, 128), F32),
            pltpu.VMEM((channels // 4, 2 * NF, TILE), BF16),
            pltpu.VMEM(mine.shape, BF16),
            pltpu.VMEM(theirs.shape, BF16),
            pltpu.VMEM(own.shape, F32),
            pltpu.VMEM(table.shape, BF16),
            pltpu.SemaphoreType.DMA((4,)),
        ],
        compiler_params=pltpu.CompilerParams(vmem_limit_bytes=VMEM_LIMIT),
        name="correlate",
    )(mine, theirs, own, table, place, order)


def finish_kernel(scale, place_ref, *refs):
    parts, out_ref = refs[:-1], refs[-1]
    segs = parts[0].shape[0]
    pairs = out_ref.shape[0] // 2
    rows = parts[0].shape[1] // pairs
    block = out_ref.shape[1]
    for i in range(pairs):
        stacked = jnp.concatenate(
            [part[g, i * rows : (i + 1) * rows, :] for g in range(segs) for part in parts], axis=0
        )
        total = jnp.dot(place_ref[...], stacked, preferred_element_type=F32) * scale
        out_ref[2 * i : 2 * i + 2] = total.reshape(2, block, LAGS)


def finish(parts, place, scale, block, channels):
    segs, rows, _ = parts[0].shape
    step = math.gcd(channels, 16)
    piece = pl.BlockSpec((segs, rows * step // channels, LAGS), lambda i: (0, i, 0))
    return pl.pallas_call(
        functools.partial(finish_kernel, scale),
        grid=(channels // step,),
        in_specs=[pl.BlockSpec(place.shape, lambda i: (0, 0))] + [piece] * len(parts),
        out_specs=pl.BlockSpec((step, block, LAGS), lambda i: (i, 0, 0)),
        out_shape=jax.ShapeDtypeStruct((channels, block, LAGS), F32),
        compiler_params=pltpu.CompilerParams(vmem_limit_bytes=VMEM_LIMIT),
        name="finish",
    )(place, *parts)


def round_up(value, step):
    return -(-value // step) * step


def plan(source_channel, chips, chip_channels, segs):
    count = source_channel.shape[0]
    block = count // segs
    chip = source_channel // chip_channels
    index = jnp.arange(count, dtype=jnp.int32)
    seg = index // block
    same_seg = seg[:, None] == seg[None, :]
    earlier = index[None, :] < index[:, None]
    same_chip = chip[:, None] == chip[None, :]
    ahead = same_seg & ((chip[None, :] < chip[:, None]) | (same_chip & earlier))
    position = jnp.sum(ahead.astype(jnp.int32), axis=1)
    turns = np.array(
        [(0,) + t for t in itertools.product(range(CLASSES), repeat=segs - 1)], np.int32
    )
    turned = jnp.asarray(np.repeat(turns, block, axis=1))
    classes = (position[None, :] + turned) % CLASSES
    of_class = classes[:, None, :] == jnp.arange(CLASSES, dtype=jnp.int32)[None, :, None]
    of_chip = chip[:, None] == jnp.arange(chips, dtype=jnp.int32)[None, :]
    held = jnp.einsum(
        "rqs,sz->rqz", of_class.astype(BF16), of_chip.astype(BF16), preferred_element_type=F32
    )
    fullest = jnp.max(held, axis=(1, 2))
    best = jnp.argmin(fullest)
    chosen = lax.dynamic_index_in_dim(classes, best, 0, keepdims=False)
    same_class = chosen[:, None] == chosen[None, :]
    place = jnp.sum(
        (same_seg & same_class & (position[None, :] < position[:, None])).astype(jnp.int32), axis=1
    )
    slot = jnp.sum((same_chip & same_class & earlier).astype(jnp.int32), axis=1)
    return chip, chosen, place, slot, seg, jnp.min(fullest)


def on_device(strain_rate, window_length, source_channel):
    chan_index = lax.axis_index("chan")
    seg_index = lax.axis_index("seg")
    devices = lax.axis_size("chan")
    segs = lax.axis_size("seg")
    chips = devices // 2
    windows, all_channels, samples = strain_rate.shape
    channels = all_channels // devices
    per_core = windows // 2
    count = source_channel.shape[0]
    block = count // segs
    group = block // CLASSES
    spots = segs * group
    my_chip = chan_index // 2
    my_core = (chan_index % 2).astype(jnp.int32).reshape(1)

    start = (chan_index * samples).astype(jnp.int32).reshape(1)
    packed = pack(strain_rate, window_length, start, chips)
    packed = packed.reshape(devices, 2 * per_core * channels, samples)
    received = lax.all_to_all(packed, "chan", split_axis=0, concat_axis=0, tiled=True)

    chip, chosen, place, slot, seg, fullest = plan(source_channel, chips, 2 * channels, segs)
    lanes = round_up(per_core * -(-count // (CLASSES * chips)), 128)
    cap = lanes // per_core
    full = (fullest > cap).astype(jnp.int32)

    core_swap = [(i, i ^ 1) for i in range(devices)]
    upward = [(i, i + 2) for i in range(devices - 2)]
    downward = [(i + 2, i) for i in range(devices - 2)]
    lines = [list(range(core, devices, 2)) for core in range(2)]

    row = np.arange(2 * per_core * channels)
    row_window = (row // channels) % per_core
    row_channel = (row // (per_core * channels)) * channels + row % channels
    kinds = jnp.arange(CLASSES, dtype=jnp.int32)
    local = source_channel % (2 * channels)
    here = chip == my_chip

    seat = np.arange(lanes)
    seat_window = np.where(seat < per_core * cap, seat // cap, -1).astype(np.int32)
    seat_slot = (seat % cap).astype(np.int32)
    sits = (
        (chosen[None, None, :] == kinds[:, None, None])
        & (slot[None, None, :] == seat_slot[None, :, None])
        & here[None, None, :]
    )
    held = jnp.sum(jnp.where(sits, local[None, None, :] + 1, 0), axis=-1) - 1
    select = (
        (held[:, :, None] == row_channel[None, None, :])
        & (seat_window[:, None] == row_window[None, :])[None]
    ).astype(BF16).reshape(CLASSES * lanes, row.shape[0])

    spot_index = jnp.arange(spots, dtype=jnp.int32)
    at_spot = (
        (chosen[None, None, :] == kinds[:, None, None])
        & (seg * group + place == spot_index[:, None])[None]
    )
    spot_slot = jnp.sum(jnp.where(at_spot, slot[None, None, :], 0), axis=-1)
    spot_chip = jnp.sum(jnp.where(at_spot, chip[None, None, :], 0), axis=-1)
    spot_far = jnp.stack([(spot_chip[0] - my_chip) % chips, spot_chip[1]])
    column_window = np.repeat(np.arange(per_core), spots)
    far = np.repeat(np.arange(chips), lanes).astype(np.int32)
    placing = (
        (jnp.tile(spot_slot, (1, per_core))[:, None, :] == np.tile(seat_slot, chips)[None, :, None])
        & (jnp.tile(spot_far, (1, per_core))[:, None, :] == far[None, :, None])
        & (np.tile(seat_window, chips)[:, None] == column_window[None, :])[None]
    ).astype(BF16)

    my_chosen = lax.dynamic_slice_in_dim(chosen, seg_index * block, block)
    my_place = lax.dynamic_slice_in_dim(place, seg_index * block, block)
    width = CLASSES * 2 * group
    column = np.arange(segs * width) % width
    row_pair = np.repeat(np.arange(2), block)
    final = (
        (jnp.tile(my_chosen, 2)[:, None] == (column // (2 * group))[None, :])
        & (jnp.tile(my_place, 2)[:, None] == (column % group)[None, :])
        & (row_pair[:, None] == (column // group % 2)[None, :])
    ).astype(BF16)

    own, other, *sends = transform(received, select, my_core, lanes)
    own_other = lax.ppermute(other, "chan", core_swap)
    shape = (per_core, channels, 2 * NF)
    bins = gather_bins(own.reshape(shape), own_other.reshape(shape))

    from_below, from_above = [None] * chips, [None] * chips
    up = down = sends[0]
    for hop in range(1, chips):
        up = lax.ppermute(up, "chan", upward)
        down = lax.ppermute(down, "chan", downward)
        if hop == 2:
            up, down, bins, second = lax.optimization_barrier((up, down, bins, sends[1]))
        from_below[hop], from_above[hop] = up, down
    second = lax.all_gather(second, "chan", axis_index_groups=lines)
    merged = [sends[0]]
    for far_by in range(1, chips):
        merged.append(from_above[far_by] + from_below[chips - far_by])

    def stacks(mine, places):
        theirs = lax.ppermute(mine, "chan", core_swap)
        return correlate(bins, mine, theirs, places, segs)

    scale = 1.0 / math.sqrt(NF * windows * segs)

    def finished(lags):
        pieces = [
            lax.all_to_all(lag, "seg", split_axis=0, concat_axis=0, tiled=True) for lag in lags
        ]
        return finish(pieces, final, scale, block, channels)

    first_lag = stacks(jnp.stack(merged), placing[0])
    first_lag, second = lax.optimization_barrier((first_lag, second))
    second_lag = stacks(second, placing[1])
    seated = finished([first_lag, second_lag])

    def add_unseated(turn, total):
        out = (slot >= cap) & (turn < full)
        at = jnp.sum(jnp.where(at_spot & here & out, local[None, None, :] + 1, 0), axis=-1) - 1
        wanted = (
            (jnp.tile(at, (1, per_core))[:, :, None] == row_channel[None, None, :])
            & (np.repeat(np.arange(per_core), spots)[:, None] == row_window[None, :])[None]
        ).astype(BF16)
        spot = jnp.eye(per_core * spots, dtype=BF16)
        first = my_core[0] == 0
        white = jnp.concatenate([jnp.where(first, own, other), jnp.where(first, other, own)])
        lags = []
        for q in range(CLASSES):
            mine = jnp.einsum("sr,rk->ks", wanted[q], white, preferred_element_type=F32)
            mine = lax.psum(mine.astype(BF16), "chan", axis_index_groups=lines)
            lags.append(stacks(mine[None], spot))
        return total + finished(lags)

    _, stacked = lax.while_loop(
        lambda carry: carry[0] < full,
        lambda carry: (carry[0] + 1, add_unseated(*carry)),
        (jnp.zeros((), jnp.int32), seated),
    )
    return stacked


def solution(mesh):
    in_specs = (P("seg", None, "chan"), P("seg"), P())
    out_specs = P("chan", "seg", None)
    return jax.shard_map(
        on_device, mesh=mesh, in_specs=in_specs, out_specs=out_specs, check_vma=False
    )
```
